128 devices in a mesh: row: 8 (over z_hi, x), col: 16 (over y, z_lo, core).
Axes of the slice: x: 4, y: 4, z: 4 (z_hi: 2, z_lo: 2; z = z_hi * 2 + z_lo), core: 2. Of those that a mesh axis runs over, the one named last changes fastest.
Arguments:
- features: bfloat16 [320, 320, 2048], P('row', 'col'), may hold values from 0 to 30
- w_point: bfloat16 [2048, 128], replicated, may hold values from -0.125 to 0.125
- w_rate_six: bfloat16 [3, 3, 2048, 128], replicated, may hold values from -0.046875 to 0.046875
- w_rate_twelve: bfloat16 [3, 3, 2048, 128], replicated, may hold values from -0.046875 to 0.046875
- w_rate_eighteen: bfloat16 [3, 3, 2048, 128], replicated, may hold values from -0.046875 to 0.046875
- w_pool: bfloat16 [2048, 128], replicated, may hold values from -0.125 to 0.125
- w_proj: bfloat16 [640, 256], replicated, may hold values from -0.25 to 0.25
Outputs:
- head_out: bfloat16 [320, 320, 256], P('row', 'col')
The draws below stay inside these ranges and needn't reach their ends.
All inputs are finite; a program needn't handle non-finite values.
Results may differ from the reference program's by a relative error of at most 0.0052.
Values may be sent and summed in bfloat16 or wider, within the bound.
A program may use at most 192 MiB of HBM per device.

```python
import jax
import jax.numpy as jnp
from jax import lax

F = 2048
BR = 128
OUT = 256
NH = 320
NW = 320


def block_scales(key, lower, upper):
    block_rows = (NH + 9) // 10
    block_cols = (NW + 9) // 10
    logs = jax.random.uniform(key, (block_rows, block_cols, F), jnp.float32, jnp.log(lower), jnp.log(upper))
    scales = jnp.exp(logs)
    scales = jnp.repeat(scales, 10, axis=0)[:NH]
    scales = jnp.repeat(scales, 10, axis=1)[:, :NW]
    return scales


def draw_features(key, part):
    key = jax.random.fold_in(key, 7)
    key_base = jax.random.fold_in(key, 1)
    key_block = jax.random.fold_in(key, 3)
    rows = jnp.arange(NH, dtype=jnp.float32) / NH
    cols = jnp.arange(NW, dtype=jnp.float32) / NW
    ramp = 1.0 + rows[:, None] + cols[None, :]
    blocks = block_scales(key_block, 0.3, 3.0)
    base = jnp.clip(jnp.abs(jax.random.normal(key_base, (NH, NW, F), jnp.float32)), 0.0, 3.0)
    values = base * blocks * ramp[:, :, None]
    return values.astype(jnp.bfloat16)


def scatter_about(stream_key, dims, width, limit, held_as=jnp.bfloat16):
    values = jax.random.normal(stream_key, dims, jnp.float32) * width
    return jnp.minimum(jnp.maximum(values, -limit), limit).astype(held_as)


def setup_inputs(seed: int = 0) -> dict:
    seeds = jax.random.split(jax.random.key(seed), 8)
    return {
        "features": draw_features(jax.random.fold_in(seeds[7], 71), 0),
        "w_point": scatter_about(seeds[1], (F, BR), F ** -0.5, 0.125),
        "w_rate_six": scatter_about(seeds[2], (3, 3, F, BR), (9 * F) ** -0.5, 0.046875),
        "w_rate_twelve": scatter_about(seeds[3], (3, 3, F, BR), (9 * F) ** -0.5, 0.046875),
        "w_rate_eighteen": scatter_about(seeds[4], (3, 3, F, BR), (9 * F) ** -0.5, 0.046875),
        "w_pool": scatter_about(seeds[5], (F, BR), F ** -0.5, 0.125),
        "w_proj": scatter_about(seeds[6], (5 * BR, OUT), (5 * BR) ** -0.5, 0.25),
    }


def atrous(features, kernel, rate):
    out = lax.conv_general_dilated(
        features.astype(jnp.float32)[None], kernel.astype(jnp.float32), (1, 1),
        [(rate, rate), (rate, rate)], rhs_dilation=(rate, rate),
        dimension_numbers=("NHWC", "HWIO", "NHWC"))[0]
    return jax.nn.relu(out).astype(jnp.bfloat16)


def reference(features, w_point, w_rate_six, w_rate_twelve, w_rate_eighteen, w_pool, w_proj):
    point_branch = jax.nn.relu(jnp.einsum("rcf,fo->rco", features.astype(jnp.float32), w_point.astype(jnp.float32))).astype(jnp.bfloat16)
    branches = [point_branch]
    for rate, kernel in ((6, w_rate_six), (12, w_rate_twelve), (18, w_rate_eighteen)):
        branches.append(atrous(features, kernel, rate))
    total = jnp.sum(features, axis=(0, 1), dtype=jnp.float32)
    pooled = (total / (NH * NW)).astype(jnp.bfloat16)
    pool_branch = jax.nn.relu(jnp.dot(pooled[None], w_pool, preferred_element_type=jnp.float32)).astype(jnp.bfloat16)
    branches.append(jnp.broadcast_to(pool_branch[None], (NH, NW, pool_branch.shape[1])))
    joined = jnp.concatenate(branches, axis=-1)
    mixed = jnp.einsum("rck,ko->rco", joined.astype(jnp.float32), w_proj.astype(jnp.float32))
    return jax.nn.relu(mixed).astype(jnp.bfloat16)
```

```python
import functools

import jax
import jax.numpy as jnp
from jax import lax
from jax.experimental import pallas as pl
from jax.experimental.pallas import tpu as pltpu
from jax.sharding import PartitionSpec as P

MESH = pl.DeviceIdType.MESH
BF = jnp.bfloat16
F32 = jnp.float32
RATES = (18, 12, 6)
ROWS, COLS, BR, OUT = 40, 20, 128, 256
PIX = ROWS * COLS
GROUP = 8
SPAN = GROUP * COLS


def up16(n):
    return -(-n // 16) * 16


def body(
    n_row, n_col,
    x_hbm, wp_hbm, w6_hbm, w12_hbm, w18_hbm, wpool_hbm, wproj_hbm,
    out_ref,
    xraw, xc, w18, w12, w6, wp, wpool, wproj,
    z18, z12, z6, point,
    su18, su12, su6, sd18, sd12, sd6, ru18, ru12, ru6, rd18, rd12, rd6,
    sl18, sl12, sl6, sr18, sr12, sr6, rl18, rl12, rl6, rr18, rr12, rr6,
    psum, prow, pcol, poolrow,
    xsem, wsem, wsem2, row_ss, row_rs, col_ss, col_rs, pr_ss, pr_rs, pc_ss, pc_rs,
):
    r = lax.axis_index("row")
    c = lax.axis_index("col")
    has_up, has_down = r > 0, r < n_row - 1
    has_left, has_right = c > 0, c < n_col - 1
    up, down = lax.rem(r + n_row - 1, n_row), lax.rem(r + 1, n_row)
    left, right = lax.rem(c + n_col - 1, n_col), lax.rem(c + 1, n_col)

    W = {18: w18, 12: w12, 6: w6}
    Z = {18: z18, 12: z12, 6: z6}
    SU, SD = {18: su18, 12: su12, 6: su6}, {18: sd18, 12: sd12, 6: sd6}
    RU, RD = {18: ru18, 12: ru12, 6: ru6}, {18: rd18, 12: rd12, 6: rd6}
    SL, SR = {18: sl18, 12: sl12, 6: sl6}, {18: sr18, 12: sr12, 6: sr6}
    RL, RR = {18: rl18, 12: rl12, 6: rl6}, {18: rr18, 12: rr12, 6: rr6}

    xcopies = []
    for i in range(5):
        cp = pltpu.make_async_copy(x_hbm.at[pl.ds(8 * i, 8)], xraw.at[pl.ds(8 * i, 8)], xsem.at[i])
        cp.start()
        xcopies.append(cp)
    wcopies = {}
    for n, (d, hbm) in enumerate(((18, w18_hbm), (12, w12_hbm), (6, w6_hbm))):
        for m, a in enumerate((0, 2, 1)):
            cp = pltpu.make_async_copy(hbm.at[a], W[d].at[a], wsem.at[3 * n + m])
            cp.start()
            wcopies[d, a] = cp
    tail = []
    for i, (s, t) in enumerate(((wp_hbm, wp), (wpool_hbm, wpool), (wproj_hbm, wproj))):
        cp = pltpu.make_async_copy(s, t, wsem2.at[i])
        cp.start()
        tail.append(cp)

    barrier = pltpu.get_barrier_semaphore()
    for k in range(1, n_row):
        pl.semaphore_signal(barrier, inc=1, device_id=(lax.rem(r + k, n_row), c), device_id_type=MESH)
    for k in range(1, n_col):
        pl.semaphore_signal(barrier, inc=1, device_id=(r, lax.rem(c + k, n_col)), device_id_type=MESH)

    psum[...] = jnp.zeros_like(psum)
    for i in range(5):
        xcopies[i].wait()
        for h in range(2):
            rows = [xraw[8 * i + 4 * h + k].astype(F32) for k in range(4)]
            flat = jnp.concatenate(rows, axis=0)
            n = 4 * COLS
            base = (2 * i + h) * n
            xc[base : base + n] = flat.astype(BF)
            part = flat[0:8]
            for k in range(1, n // 8):
                part = part + flat[8 * k : 8 * k + 8]
            psum[...] += part

    chans = xc.shape[1]
    lanes = chans // BR
    total = jnp.sum(psum[...], axis=0, keepdims=True)
    prow[0] = jnp.concatenate([total[:, BR * k : BR * k + BR] for k in range(lanes)], axis=0)
    pl.semaphore_wait(barrier, n_row + n_col - 2)

    def pool_row(k):
        return pltpu.make_async_remote_copy(
            src_ref=prow.at[0], dst_ref=prow.at[k], send_sem=pr_ss.at[k], recv_sem=pr_rs.at[k],
            device_id=(lax.rem(r + k, n_row), c), device_id_type=MESH)

    def pool_col(k):
        return pltpu.make_async_remote_copy(
            src_ref=pcol.at[0], dst_ref=pcol.at[k], send_sem=pc_ss.at[k], recv_sem=pc_rs.at[k],
            device_id=(r, lax.rem(c + k, n_col)), device_id_type=MESH)

    for k in range(1, n_row):
        pool_row(k).start()

    def row_copy(d, way):
        n = 2 * RATES.index(d) + way
        src, dst, to = ((SU[d], RU[d], up), (SD[d], RD[d], down))[way]
        return pltpu.make_async_remote_copy(
            src_ref=src, dst_ref=dst, send_sem=row_ss.at[n], recv_sem=row_rs.at[n],
            device_id=(to, c), device_id_type=MESH)

    def col_copy(d, way):
        n = 2 * RATES.index(d) + way
        src, dst, to = ((SL[d], RR[d], left), (SR[d], RL[d], right))[way]
        return pltpu.make_async_remote_copy(
            src_ref=src, dst_ref=dst, send_sem=col_ss.at[n], recv_sem=col_rs.at[n],
            device_id=(r, to), device_id_type=MESH)

    def dot2(wa, wb):
        w = jnp.concatenate([wa, wb], axis=1)
        y = jnp.dot(xc[...], w, preferred_element_type=F32)
        return y[:, :BR], y[:, BR:]

    def off_rows(d):
        w, z = W[d], Z[d]
        edge = 2 * d * COLS
        for b in range(3):
            down_part, up_part = dot2(w[0, b], w[2, b])
            z[b, 0:PIX] = up_part
            z[b, edge:PIX] += down_part[0 : PIX - edge]
            z[b, PIX : PIX + edge] = down_part[PIX - edge : PIX]
        high = up16(d * COLS)
        size = z.shape[1]
        SU[d][...] = z[:, 0:high].astype(BF)
        SD[d][...] = z[:, size - high : size].astype(BF)

        @pl.when(has_up)
        def _():
            row_copy(d, 0).start()

        @pl.when(has_down)
        def _():
            row_copy(d, 1).start()

    def own_rows(d):
        w, z = W[d], Z[d]
        y0, y2 = dot2(w[1, 0], w[1, 2])
        z[0, d * COLS : d * COLS + PIX] += y0
        z[2, d * COLS : d * COLS + PIX] += y2

    def rows_in(d):
        z = Z[d]
        n = d * COLS
        gap = up16(n) - n

        @pl.when(has_down)
        def _():
            row_copy(d, 0).wait_recv()
            for b in range(3):
                z[b, PIX : PIX + n] += RU[d][b].astype(F32)[0:n]

        @pl.when(has_up)
        def _():
            row_copy(d, 1).wait_recv()
            for b in range(3):
                z[b, n : 2 * n] += RD[d][b].astype(F32)[gap : gap + n]

    def cols_out(d):
        z = Z[d]
        for i in range(ROWS // GROUP):
            at = d * COLS + i * SPAN
            z0 = z[0, at : at + SPAN]
            z2 = z[2, at : at + SPAN]
            SR[d][i * GROUP * d : (i + 1) * GROUP * d] = jnp.concatenate(
                [z0[COLS * k + COLS - d : COLS * k + COLS] for k in range(GROUP)], axis=0).astype(BF)
            SL[d][i * GROUP * d : (i + 1) * GROUP * d] = jnp.concatenate(
                [z2[COLS * k : COLS * k + d] for k in range(GROUP)], axis=0).astype(BF)

        @pl.when(has_left)
        def _():
            col_copy(d, 0).start()

        @pl.when(has_right)
        def _():
            col_copy(d, 1).start()

    @pl.when(jnp.logical_not(has_left))
    def _():
        for d in RATES:
            RL[d][...] = jnp.zeros_like(RL[d])

    @pl.when(jnp.logical_not(has_right))
    def _():
        for d in RATES:
            RR[d][...] = jnp.zeros_like(RR[d])

    wcopies[18, 0].wait()
    wcopies[18, 2].wait()
    off_rows(18)
    wcopies[18, 1].wait()
    own_rows(18)
    wcopies[12, 0].wait()
    wcopies[12, 2].wait()
    off_rows(12)
    rows_in(18)
    cols_out(18)
    wcopies[12, 1].wait()
    own_rows(12)

    for k in range(1, n_row):
        pool_row(k).wait_recv()
    acc = prow[0]
    for k in range(1, n_row):
        acc = acc + prow[k]
    pcol[0] = acc
    for k in range(1, n_col):
        pool_col(k).start()

    wcopies[6, 0].wait()
    wcopies[6, 2].wait()
    off_rows(6)
    rows_in(12)
    cols_out(12)
    wcopies[6, 1].wait()
    own_rows(6)
    y18, y12 = dot2(w18[1, 1], w12[1, 1])
    z18[1, 18 * COLS : 18 * COLS + PIX] += y18
    z12[1, 12 * COLS : 12 * COLS + PIX] += y12
    rows_in(6)
    cols_out(6)
    for cp in tail:
        cp.wait()
    y6, yp = dot2(w6[1, 1], wp[...])
    z6[1, 6 * COLS : 6 * COLS + PIX] += y6
    point[...] = jnp.maximum(yp, 0.0).astype(BF)

    for k in range(1, n_col):
        pool_col(k).wait_recv()
    acc = pcol[0]
    for k in range(1, n_col):
        acc = acc + pcol[k]
    pooled = (acc / (PIX * n_row * n_col)).astype(BF).astype(F32)
    flat = jnp.concatenate([pooled[k : k + 1] for k in range(lanes)], axis=1)
    flat = jnp.broadcast_to(flat, (16, chans)).astype(BF)
    branch = jnp.maximum(jnp.dot(flat, wpool[...], preferred_element_type=F32), 0.0).astype(BF)
    poolrow[...] = jnp.dot(branch, wproj[4 * BR : 5 * BR], preferred_element_type=F32)[0:8]

    for d in RATES:
        @pl.when(has_right)
        def _(d=d):
            col_copy(d, 0).wait_recv()

        @pl.when(has_left)
        def _(d=d):
            col_copy(d, 1).wait_recv()

    base_row = poolrow[0:1]
    for i in range(ROWS // GROUP):
        at = i * SPAN
        joined = [point[at : at + SPAN]]
        for d in (6, 12, 18):
            z = Z[d]
            z0, z1, z2 = (z[b, d * COLS + at : d * COLS + at + SPAN] for b in range(3))
            got_l = RL[d][i * GROUP * d : (i + 1) * GROUP * d].astype(F32)
            got_r = RR[d][i * GROUP * d : (i + 1) * GROUP * d].astype(F32)
            from_left, from_right = [], []
            for k in range(GROUP):
                from_left += [got_l[k * d : (k + 1) * d], z0[COLS * k : COLS * k + COLS - d]]
                from_right += [z2[COLS * k + d : COLS * k + COLS], got_r[k * d : (k + 1) * d]]
            whole = z1 + jnp.concatenate(from_left, axis=0) + jnp.concatenate(from_right, axis=0)
            joined.append(jnp.maximum(whole, 0.0).astype(BF))
        mixed = jnp.dot(jnp.concatenate(joined, axis=1), wproj[0 : 4 * BR], preferred_element_type=F32)
        out_ref[at : at + SPAN] = jnp.maximum(mixed + base_row, 0.0).astype(BF)

    for k in range(1, n_row):
        pool_row(k).wait_send()
    for k in range(1, n_col):
        pool_col(k).wait_send()
    for d in RATES:
        @pl.when(has_up)
        def _(d=d):
            row_copy(d, 0).wait_send()

        @pl.when(has_down)
        def _(d=d):
            row_copy(d, 1).wait_send()

        @pl.when(has_left)
        def _(d=d):
            col_copy(d, 0).wait_send()

        @pl.when(has_right)
        def _(d=d):
            col_copy(d, 1).wait_send()


def per_device(n_row, n_col, features, w_point, w_rate_six, w_rate_twelve, w_rate_eighteen, w_pool, w_proj):
    chans = features.shape[2]
    lanes = chans // BR
    vm = pltpu.VMEM
    dma = pltpu.SemaphoreType.DMA
    scratch = [vm((ROWS, COLS, chans), BF), vm((PIX, chans), BF)]
    scratch += [vm((3, 3, chans, BR), BF)] * 3
    scratch += [vm((chans, BR), BF), vm((chans, BR), BF), vm((5 * BR, OUT), BF)]
    scratch += [vm((3, PIX + 2 * d * COLS, BR), F32) for d in RATES]
    scratch += [vm((PIX, BR), BF)]
    for _ in range(4):
        scratch += [vm((3, up16(d * COLS), BR), BF) for d in RATES]
    for _ in range(4):
        scratch += [vm((ROWS * d, BR), BF) for d in RATES]
    scratch += [vm((8, chans), F32), vm((n_row, lanes, BR), F32), vm((n_col, lanes, BR), F32), vm((8, OUT), F32)]
    scratch += [dma((5,)), dma((9,)), dma((3,)), dma((6,)), dma((6,)), dma((6,)), dma((6,)),
                dma((n_row,)), dma((n_row,)), dma((n_col,)), dma((n_col,))]
    flops = 2 * PIX * chans * BR * 28 + 2 * PIX * 5 * BR * OUT
    out = pl.pallas_call(
        functools.partial(body, n_row, n_col),
        name="aspp_head",
        out_shape=jax.ShapeDtypeStruct((PIX, OUT), BF),
        in_specs=[pl.BlockSpec(memory_space=pl.ANY)] * 7,
        out_specs=pl.BlockSpec(memory_space=pltpu.VMEM),
        scratch_shapes=scratch,
        compiler_params=pltpu.CompilerParams(
            collective_id=0, has_side_effects=True, vmem_limit_bytes=58 << 20),
        cost_estimate=pl.CostEstimate(flops=flops, bytes_accessed=20 << 20, transcendentals=0),
    )(features, w_point, w_rate_six, w_rate_twelve, w_rate_eighteen, w_pool, w_proj)
    return out.reshape(ROWS, COLS, OUT)


def solution(mesh):
    placed = (P("row", "col", None), P(), P(), P(), P(), P(), P())
    return jax.shard_map(
        functools.partial(per_device, mesh.shape["row"], mesh.shape["col"]),
        mesh=mesh, in_specs=placed, out_specs=P("row", "col", None), check_vma=False)
```

```python
import functools

import jax
import jax.numpy as jnp
from jax import lax
from jax.experimental import pallas as pl
from jax.experimental.pallas import tpu as pltpu
from jax.sharding import PartitionSpec as P

MESH = pl.DeviceIdType.MESH
BF = jnp.bfloat16
F32 = jnp.float32
RATES = (18, 12, 6)
ROWS, COLS, BR, OUT = 40, 20, 128, 256
PIX = ROWS * COLS
PACK = {18: 8, 12: 4, 6: 8}
XPARTS = 5
STEPS, TAPS = 7, 4
PLANE = {d: PIX + 2 * d * ROWS for d in RATES}
BASE = {18: 0, 12: 3 * PLANE[18], 6: 3 * (PLANE[18] + PLANE[12])}
POINT = 3 * (PLANE[18] + PLANE[12] + PLANE[6])


def up16(n):
    return -(-n // 16) * 16


def take(buf, start, stop):
    low, high = start // 16 * 16, up16(stop)
    return buf[low:high].astype(F32)[start - low : stop - low]


def taps_of(step):
    if step == STEPS - 1:
        return [(18, 1, 1), (12, 1, 1), (6, 1, 1), None]
    d = RATES[step // 2]
    pairs = [(0, 2), (2, 2), (0, 0), (2, 0)] if step % 2 == 0 else [(0, 1), (2, 1), (1, 2), (1, 0)]
    return [(d, a, b) for a, b in pairs]


def places(step):
    i, odd, last = step // 2, step % 2, step // (STEPS - 1)
    s = 18 * ROWS - 6 * ROWS * i
    plane = PIX + 2 * s
    base = 3 * PLANE[18] * i - 3 * 6 * ROWS * i * (i - 1)
    even = [base, base + 2 * plane, base + 2 * s, base + 2 * plane + 2 * s]
    uneven = [base + s, base + 2 * plane + s, base + plane, base + plane + 2 * s]
    end = [BASE[d] + PLANE[d] + ROWS * d for d in RATES] + [POINT]
    return [(1 - last) * ((1 - odd) * e + odd * u) + last * z for e, u, z in zip(even, uneven, end)]


def body(
    n_row, n_col,
    x_hbm, wp_hbm, w6_hbm, w12_hbm, w18_hbm, wpool_hbm,
    joined,
    x, w, wpool, z,
    cu18, cu12, cu6, cd18, cd12, cd6, hu18, hu12, hu6, hd18, hd12, hd6,
    gcu18, gcu12, gcu6, gcd18, gcd12, gcd6, ghu18, ghu12, ghu6, ghd18, ghd12, ghd6,
    sl18, sl12, sl6, sr18, sr12, sr6, rl18, rl12, rl6, rr18, rr12, rr6,
    prow, pcol,
    xsem, wsem, wpsem, row_ss, row_rs, own_ss, own_rs, col_ss, col_rs, pr_ss, pr_rs, pc_ss, pc_rs,
):
    r = lax.axis_index("row")
    c = lax.axis_index("col")
    has_up, has_down = r > 0, r < n_row - 1
    has_left, has_right = c > 0, c < n_col - 1
    up, down = lax.rem(r + n_row - 1, n_row), lax.rem(r + 1, n_row)
    left, right = lax.rem(c + n_col - 1, n_col), lax.rem(c + 1, n_col)

    by = lambda *bufs: dict(zip(RATES, bufs))
    CU, CD, HU, HD = by(cu18, cu12, cu6), by(cd18, cd12, cd6), by(hu18, hu12, hu6), by(hd18, hd12, hd6)
    GCU, GCD = by(gcu18, gcu12, gcu6), by(gcd18, gcd12, gcd6)
    GHU, GHD = by(ghu18, ghu12, ghu6), by(ghd18, ghd12, ghd6)
    SL, SR, RL, RR = by(sl18, sl12, sl6), by(sr18, sr12, sr6), by(rl18, rl12, rl6), by(rr18, rr12, rr6)
    RATE_HBM = {18: w18_hbm, 12: w12_hbm, 6: w6_hbm}

    def start_weights(step):
        for k, tap in enumerate(taps_of(step)):
            src = wp_hbm if tap is None else RATE_HBM[tap[0]].at[tap[1], tap[2]]
            pltpu.make_async_copy(src, w.at[step, k], wsem.at[step]).start()

    start_weights(0)
    xcopies = []
    part = PIX // XPARTS
    for i in range(XPARTS):
        cp = pltpu.make_async_copy(x_hbm.at[pl.ds(part * i, part)], x.at[pl.ds(part * i, part)], xsem.at[i])
        cp.start()
        xcopies.append(cp)
    pool_weights = pltpu.make_async_copy(wpool_hbm, wpool, wpsem.at[0])

    barrier = pltpu.get_barrier_semaphore()
    for k in range(1, n_row):
        pl.semaphore_signal(barrier, inc=1, device_id=(lax.rem(r + k, n_row), c), device_id_type=MESH)
    for k in range(1, n_col):
        pl.semaphore_signal(barrier, inc=1, device_id=(r, lax.rem(c + k, n_col)), device_id_type=MESH)

    for there, bufs in ((has_up, (GCD, GHD)), (has_down, (GCU, GHU)), (has_left, (RL,)), (has_right, (RR,))):
        @pl.when(jnp.logical_not(there))
        def _(bufs=bufs):
            for buf in bufs:
                for d in RATES:
                    buf[d][...] = jnp.zeros_like(buf[d])

    @pl.loop(0, z.shape[0] // 160)
    def _(i):
        z[pl.ds(pl.multiple_of(i * 160, 160), 160)] = jnp.zeros((160, BR), F32)

    chans = x.shape[1]
    lanes = chans // BR
    acc = jnp.zeros((8, chans), F32)
    for i in range(XPARTS):
        xcopies[i].wait()

        def add(k, acc, i=i):
            at = pl.multiple_of(part * i + 16 * k, 16)
            rows = x[pl.ds(at, 16)].astype(F32)
            return acc + (rows[0:8] + rows[8:16])

        acc = lax.fori_loop(0, part // 16, add, acc)
    total = jnp.sum(acc, axis=0, keepdims=True)
    prow[0] = jnp.concatenate([total[:, BR * k : BR * k + BR] for k in range(lanes)], axis=0)
    start_weights(1)
    start_weights(2)

    def pool_row(k):
        return pltpu.make_async_remote_copy(
            src_ref=prow.at[0], dst_ref=prow.at[k], send_sem=pr_ss.at[k], recv_sem=pr_rs.at[k],
            device_id=(lax.rem(r + k, n_row), c), device_id_type=MESH)

    def pool_col(k):
        return pltpu.make_async_remote_copy(
            src_ref=pcol.at[0], dst_ref=pcol.at[k], send_sem=pc_ss.at[k], recv_sem=pc_rs.at[k],
            device_id=(r, lax.rem(c + k, n_col)), device_id_type=MESH)

    def corner_copy(d, way):
        n = 2 * RATES.index(d) + way
        src, dst, to = ((CU[d], GCU[d], up), (CD[d], GCD[d], down))[way]
        return pltpu.make_async_remote_copy(
            src_ref=src, dst_ref=dst, send_sem=row_ss.at[n], recv_sem=row_rs.at[n],
            device_id=(to, c), device_id_type=MESH)

    def own_copy(d, way):
        n = 2 * RATES.index(d) + way
        src, dst, to = ((HU[d], GHU[d], up), (HD[d], GHD[d], down))[way]
        return pltpu.make_async_remote_copy(
            src_ref=src, dst_ref=dst, send_sem=own_ss.at[n], recv_sem=own_rs.at[n],
            device_id=(to, c), device_id_type=MESH)

    def col_copy(d, way):
        n = 2 * RATES.index(d) + way
        src, dst, to = ((SL[d], RR[d], left), (SR[d], RL[d], right))[way]
        return pltpu.make_async_remote_copy(
            src_ref=src, dst_ref=dst, send_sem=col_ss.at[n], recv_sem=col_rs.at[n],
            device_id=(r, to), device_id_type=MESH)

    def start(copy, d, first, second):
        @pl.when(first)
        def _():
            copy(d, 0).start()

        @pl.when(second)
        def _():
            copy(d, 1).start()

    def arrive(copy, d, first, second):
        @pl.when(first)
        def _():
            copy(d, 0).wait_recv()

        @pl.when(second)
        def _():
            copy(d, 1).wait_recv()

    def pack(d, columns, to_up, to_down):
        g = PACK[d]
        for k in range(0, len(columns), g):
            some = columns[k : k + g]
            gap = [jnp.zeros((up16(len(some) * d) - len(some) * d, BR), F32)] if len(some) * d % 16 else []
            at2 = BASE[d] + 2 * PLANE[d]
            at0 = BASE[d]
            rows = slice(k * d, k * d + up16(len(some) * d))
            to_up[rows] = jnp.concatenate(
                [z[at2 + ROWS * j : at2 + ROWS * (j + 1)][0:d] for j in some] + gap, axis=0).astype(BF)
            to_down[rows] = jnp.concatenate(
                [z[at0 + ROWS * j : at0 + ROWS * (j + 1)][ROWS - d : ROWS] for j in some] + gap, axis=0).astype(BF)

    def corners_out(d):
        pack(d, list(range(d)) + list(range(d + COLS, COLS + 2 * d)), CU[d], CD[d])
        start(corner_copy, d, has_up, has_down)

    def own_out(d):
        pack(d, list(range(d, d + COLS)), HU[d], HD[d])
        start(own_copy, d, has_up, has_down)

    def summed(d, first, count, got_u, got_d, k):
        z0, z1, z2 = (z[BASE[d] + a * PLANE[d] + ROWS * first : BASE[d] + a * PLANE[d] + ROWS * (first + count)]
                      for a in range(3))
        got_u = take(got_u, k * d, (k + count) * d)
        got_d = take(got_d, k * d, (k + count) * d)
        above, below = [], []
        for k in range(count):
            above += [got_d[k * d : (k + 1) * d], z0[ROWS * k : ROWS * (k + 1) - d]]
            below += [z2[ROWS * k + d : ROWS * (k + 1)], got_u[k * d : (k + 1) * d]]
        return z1 + jnp.concatenate(above, axis=0) + jnp.concatenate(below, axis=0)

    def cols_out(d):
        arrive(corner_copy, d, has_down, has_up)
        for k in range(0, d, 6):
            rows = slice(ROWS * k, ROWS * (k + 6))
            SL[d][rows] = summed(d, k, 6, GCU[d], GCD[d], k).astype(BF)
            SR[d][rows] = summed(d, COLS + d + k, 6, GCU[d], GCD[d], d + k).astype(BF)
        start(col_copy, d, has_left, has_right)

    def own_in(d):
        arrive(own_copy, d, has_down, has_up)
        for k in range(0, COLS, 4):
            at = BASE[d] + PLANE[d] + ROWS * (d + k)
            z[at : at + 4 * ROWS] = summed(d, d + k, 4, GHU[d], GHD[d], k)

    def pool_first():
        for k in range(1, n_row):
            pool_row(k).start()

    def pool_second():
        for k in range(1, n_row):
            pool_row(k).wait_recv()
        acc = prow[0]
        for k in range(1, n_row):
            acc = acc + prow[k]
        pcol[0] = acc
        for k in range(1, n_col):
            pool_col(k).start()

    def pool_third():
        for k in range(1, n_col):
            pool_col(k).wait_recv()
        acc = pcol[0]
        for k in range(1, n_col):
            acc = acc + pcol[k]
        pooled = (acc / (PIX * n_row * n_col)).astype(BF).astype(F32)
        pool_weights.wait()
        side = jnp.transpose(pooled, (1, 0))
        parts = jnp.zeros((8, BR), F32)
        for k in range(lanes):
            prod = side[:, k : k + 1] * wpool[BR * k : BR * k + BR].astype(F32)
            parts = parts + jnp.sum(prod.reshape(BR // 8, 8, BR), axis=0)
        branch = jnp.maximum(jnp.sum(parts, axis=0, keepdims=True), 0.0)
        joined[:, 4 * BR : 5 * BR] = jnp.broadcast_to(branch, (PIX, BR)).astype(BF)

    def after(step):
        if step == 0:
            pl.semaphore_wait(barrier, n_row + n_col - 2)
            corners_out(18)
            pool_first()
            start_weights(3)
        elif step == 1:
            start_weights(4)
            own_out(18)
        elif step == 2:
            corners_out(12)
            start_weights(5)
            pool_second()
        elif step == 3:
            start_weights(6)
            pool_weights.start()
            cols_out(18)
            own_out(12)
        elif step == 4:
            corners_out(6)
            cols_out(12)
        elif step == 5:
            own_out(6)
            cols_out(6)
            pool_third()

    @pl.loop(0, STEPS)
    def _(step):
        pltpu.make_async_copy(w.at[step], w.at[step], wsem.at[step]).wait()
        taps = jnp.concatenate([w[step, k] for k in range(TAPS)], axis=1)
        y = jnp.dot(x[...], taps, preferred_element_type=F32)
        for k, at in enumerate(places(step)):
            rows = pl.ds(pl.multiple_of(at, 8), PIX)
            z[rows] += y[:, BR * k : BR * k + BR]
        for s in range(STEPS - 1):
            @pl.when(step == s)
            def _(s=s):
                after(s)

    joined[:, 0:BR] = jnp.maximum(z[POINT : POINT + PIX], 0.0).astype(BF)
    for d in RATES:
        own_in(d)
    for n, d in ((3, 18), (2, 12), (1, 6)):
        arrive(col_copy, d, has_right, has_left)
        at = BASE[d] + PLANE[d] + ROWS * d
        for k in range(0, COLS, 2):
            whole = z[at + ROWS * k : at + ROWS * (k + 2)]
            if k < d:
                whole = whole + RL[d][ROWS * k : ROWS * (k + 2)].astype(F32)
            if k >= COLS - d:
                j = k - (COLS - d)
                whole = whole + RR[d][ROWS * j : ROWS * (j + 2)].astype(F32)
            joined[ROWS * k : ROWS * (k + 2), BR * n : BR * (n + 1)] = jnp.maximum(whole, 0.0).astype(BF)

    for k in range(1, n_row):
        pool_row(k).wait_send()
    for k in range(1, n_col):
        pool_col(k).wait_send()
    for d in RATES:
        for there, copy in (
            (has_up, corner_copy(d, 0)), (has_down, corner_copy(d, 1)), (has_up, own_copy(d, 0)),
            (has_down, own_copy(d, 1)), (has_left, col_copy(d, 0)), (has_right, col_copy(d, 1)),
        ):
            @pl.when(there)
            def _(copy=copy):
                copy.wait_send()


def per_device(n_row, n_col, features, w_point, w_rate_six, w_rate_twelve, w_rate_eighteen, w_pool, w_proj):
    chans = features.shape[2]
    lanes = chans // BR
    vm = pltpu.VMEM
    dma = pltpu.SemaphoreType.DMA
    scratch = [vm((PIX, chans), BF), vm((STEPS, TAPS, chans, BR), BF), vm((chans, BR), BF), vm((POINT + PIX, BR), F32)]
    for _ in range(2):
        for _ in range(2):
            scratch += [vm((up16(2 * d * d), BR), BF) for d in RATES]
        for _ in range(2):
            scratch += [vm((up16(COLS * d), BR), BF) for d in RATES]
    for _ in range(4):
        scratch += [vm((ROWS * d, BR), BF) for d in RATES]
    scratch += [vm((n_row, lanes, BR), F32), vm((n_col, lanes, BR), F32)]
    scratch += [dma((XPARTS,)), dma((STEPS,)), dma((1,))] + [dma((6,))] * 6
    scratch += [dma((n_row,)), dma((n_row,)), dma((n_col,)), dma((n_col,))]
    pixels = jnp.transpose(features, (1, 0, 2)).reshape(PIX, chans)
    joined = pl.pallas_call(
        functools.partial(body, n_row, n_col),
        name="aspp_branches",
        out_shape=jax.ShapeDtypeStruct((PIX, 5 * BR), BF),
        in_specs=[pl.BlockSpec(memory_space=pl.ANY)] * 6,
        out_specs=pl.BlockSpec(memory_space=pltpu.VMEM),
        scratch_shapes=scratch,
        compiler_params=pltpu.CompilerParams(
            collective_id=0, has_side_effects=True, vmem_limit_bytes=58 << 20),
        cost_estimate=pl.CostEstimate(
            flops=2 * PIX * chans * BR * 28, bytes_accessed=20 << 20, transcendentals=0),
    )(pixels, w_point, w_rate_six, w_rate_twelve, w_rate_eighteen, w_pool)
    mixed = jnp.dot(joined, w_proj, preferred_element_type=F32)
    out = jnp.maximum(mixed, 0.0).astype(BF)
    return jnp.transpose(out.reshape(COLS, ROWS, OUT), (1, 0, 2))


def solution(mesh):
    placed = (P("row", "col", None), P(), P(), P(), P(), P(), P())
    return jax.shard_map(
        functools.partial(per_device, mesh.shape["row"], mesh.shape["col"]),
        mesh=mesh, in_specs=placed, out_specs=P("row", "col", None), check_vma=False)
```

```python
import functools

import jax
import jax.numpy as jnp
from jax import lax
from jax.experimental import pallas as pl
from jax.experimental.pallas import tpu as pltpu
from jax.sharding import PartitionSpec as P

MESH = pl.DeviceIdType.MESH
BF = jnp.bfloat16
F32 = jnp.float32
RATES = (18, 12, 6)
ROWS, COLS, BR, OUT = 40, 20, 128, 256
PIX = ROWS * COLS
PACK = {18: 8, 12: 4, 6: 8}
XPARTS = 5
STEPS, TAPS = 7, 4
PLANE = {d: COLS + 2 * d for d in RATES}
BASE = {18: 0, 12: 3 * PLANE[18], 6: 3 * (PLANE[18] + PLANE[12])}
POINT = 3 * (PLANE[18] + PLANE[12] + PLANE[6])


def up16(n):
    return -(-n // 16) * 16


def up8(n):
    return -(-n // 8) * 8


def take(buf, start, stop):
    low, high = start // 16 * 16, up16(stop)
    return buf[low:high].astype(F32)[start - low : stop - low]


def taps_of(step):
    if step == STEPS - 1:
        return [(18, 1, 1), (12, 1, 1), (6, 1, 1), None]
    d = RATES[step // 2]
    pairs = [(0, 2), (2, 2), (0, 0), (2, 0)] if step % 2 == 0 else [(0, 1), (2, 1), (1, 2), (1, 0)]
    return [(d, a, b) for a, b in pairs]


def body(
    n_row, n_col,
    x_hbm, wp_hbm, w6_hbm, w12_hbm, w18_hbm, wpool_hbm, wproj_hbm,
    out_ref,
    x, w, wpool, wproj, z, joined,
    cu18, cu12, cu6, cd18, cd12, cd6, gcu18, gcu12, gcu6, gcd18, gcd12, gcd6,
    hu18, hu12, hu6, hd18, hd12, hd6, ghu18, ghu12, ghu6, ghd18, ghd12, ghd6,
    so18, so12, so6, si18, si12, si6, ro18, ro12, ro6, ri18, ri12, ri6,
    iu18, iu12, iu6, id18, id12, id6,
    prow, pcol,
    xsem, wsem, wpsem, row_ss, row_rs, own_ss, own_rs, col_ss, col_rs, in_ss, in_rs, pr_ss, pr_rs, pc_ss, pc_rs,
):
    r = lax.axis_index("row")
    c = lax.axis_index("col")
    core = lax.rem(c, 2)
    has_up, has_down = r > 0, r < n_row - 1
    has_outer = jnp.logical_and(c > 0, c < n_col - 1)
    up, down = lax.rem(r + n_row - 1, n_row), lax.rem(r + 1, n_row)
    outer, inner = lax.rem(c + n_col - 1 + 2 * core, n_col), c + 1 - 2 * core

    by = lambda *bufs: dict(zip(RATES, bufs))
    CU, CD, GCU, GCD = by(cu18, cu12, cu6), by(cd18, cd12, cd6), by(gcu18, gcu12, gcu6), by(gcd18, gcd12, gcd6)
    HU, HD, GHU, GHD = by(hu18, hu12, hu6), by(hd18, hd12, hd6), by(ghu18, ghu12, ghu6), by(ghd18, ghd12, ghd6)
    SO, SI, RO, RI = by(so18, so12, so6), by(si18, si12, si6), by(ro18, ro12, ro6), by(ri18, ri12, ri6)
    IU, ID = by(iu18, iu12, iu6), by(id18, id12, id6)
    RATE_HBM = {18: w18_hbm, 12: w12_hbm, 6: w6_hbm}

    def start_weights(step):
        for k, tap in enumerate(taps_of(step)):
            src = wp_hbm if tap is None else RATE_HBM[tap[0]].at[tap[1], tap[2]]
            pltpu.make_async_copy(src, w.at[step, k], wsem.at[step]).start()

    start_weights(0)
    xcopies = []
    part = PIX // XPARTS
    for i in range(XPARTS):
        cp = pltpu.make_async_copy(x_hbm.at[pl.ds(part * i, part)], x.at[pl.ds(part * i, part)], xsem.at[i])
        cp.start()
        xcopies.append(cp)
    late = [pltpu.make_async_copy(wpool_hbm, wpool, wpsem.at[0]), pltpu.make_async_copy(wproj_hbm, wproj, wpsem.at[1])]

    barrier = pltpu.get_barrier_semaphore()
    for k in range(1, n_row):
        pl.semaphore_signal(barrier, inc=1, device_id=(lax.rem(r + k, n_row), c), device_id_type=MESH)
    for k in range(1, n_col):
        pl.semaphore_signal(barrier, inc=1, device_id=(r, lax.rem(c + k, n_col)), device_id_type=MESH)

    for there, bufs in ((has_up, (GCD, GHD)), (has_down, (GCU, GHU)), (has_outer, (RO,))):
        @pl.when(jnp.logical_not(there))
        def _(bufs=bufs):
            for buf in bufs:
                for d in RATES:
                    buf[d][...] = jnp.zeros_like(buf[d])

    chans = x.shape[1]
    lanes = chans // BR
    acc = jnp.zeros((8, chans), F32)
    for i in range(XPARTS):
        xcopies[i].wait()

        def add(k, acc, i=i):
            at = pl.multiple_of(part * i + 16 * k, 16)
            rows = x[pl.ds(at, 16)].astype(F32)
            return acc + (rows[0:8] + rows[8:16])

        acc = lax.fori_loop(0, part // 16, add, acc)
    total = jnp.sum(acc, axis=0, keepdims=True)
    prow[0] = jnp.concatenate([total[:, BR * k : BR * k + BR] for k in range(lanes)], axis=0)
    start_weights(1)
    start_weights(2)

    def remote(src, dst, sems, n, to):
        return pltpu.make_async_remote_copy(
            src_ref=src, dst_ref=dst, send_sem=sems[0].at[n], recv_sem=sems[1].at[n],
            device_id=to, device_id_type=MESH)

    def pool_row(k):
        return remote(prow.at[0], prow.at[k], (pr_ss, pr_rs), k, (lax.rem(r + k, n_row), c))

    def pool_col(k):
        return remote(pcol.at[0], pcol.at[k], (pc_ss, pc_rs), k, (r, lax.rem(c + k, n_col)))

    def corner_copies(d):
        n = 2 * RATES.index(d)
        return (lambda: remote(CU[d], GCU[d], (row_ss, row_rs), n, (up, c)),
                lambda: remote(CD[d], GCD[d], (row_ss, row_rs), n + 1, (down, c)))

    def own_copies(d):
        n = 2 * RATES.index(d)
        return (lambda: remote(HU[d], GHU[d], (own_ss, own_rs), n, (up, c)),
                lambda: remote(HD[d], GHD[d], (own_ss, own_rs), n + 1, (down, c)))

    def side_copies(d):
        n = 2 * RATES.index(d)
        return (lambda: remote(SO[d], RO[d], (col_ss, col_rs), n, (r, outer)),
                lambda: remote(SI[d], RI[d], (col_ss, col_rs), n + 1, (r, inner)))

    def inner_copies(d):
        n = 2 * RATES.index(d)
        high = up8(d)
        at = (1 - core) * (COLS + d)
        src_u = z.at[pl.ds(BASE[d] + 2 * PLANE[d] + at, d), pl.ds(0, high)]
        src_d = z.at[pl.ds(BASE[d] + at, d), pl.ds(ROWS - high, high)]
        return (lambda: remote(src_u, IU[d], (in_ss, in_rs), n, (r, inner)),
                lambda: remote(src_d, ID[d], (in_ss, in_rs), n + 1, (r, inner)))

    def start_rows(copies):
        @pl.when(has_up)
        def _():
            copies[0]().start()

        @pl.when(has_down)
        def _():
            copies[1]().start()

    def arrive_rows(copies):
        @pl.when(has_down)
        def _():
            copies[0]().wait_recv()

        @pl.when(has_up)
        def _():
            copies[1]().wait_recv()

    def pack(d, at, count, to_up, to_down):
        g = PACK[d]
        for k in range(0, count, g):
            n = min(g, count - k)
            gap = [jnp.zeros((up16(n * d) - n * d, BR), F32)] if n * d % 16 else []
            rows = slice(k * d, k * d + up16(n * d))
            tops = [z[BASE[d] + 2 * PLANE[d] + at + k + j][0:d] for j in range(n)]
            ends = [z[BASE[d] + at + k + j][ROWS - d : ROWS] for j in range(n)]
            to_up[rows] = jnp.concatenate(tops + gap, axis=0).astype(BF)
            to_down[rows] = jnp.concatenate(ends + gap, axis=0).astype(BF)

    def summed(d, at, count, got=None, k=0):
        if got is None:
            got_u = got_d = jnp.zeros((count * d, BR), F32)
        else:
            got_u, got_d = (take(buf[d], k * d, (k + count) * d) for buf in got)
        above, below, same = [], [], []
        for j in range(count):
            z0, z1, z2 = (z[BASE[d] + a * PLANE[d] + at + j] for a in range(3))
            above += [got_d[j * d : (j + 1) * d], z0[0 : ROWS - d]]
            below += [z2[d:ROWS], got_u[j * d : (j + 1) * d]]
            same.append(z1)
        return sum(jnp.concatenate(parts, axis=0) for parts in (same, above, below))

    def corners_out(d):
        pack(d, core * (COLS + d), d, CU[d], CD[d])
        start_rows(corner_copies(d))
        for copy in inner_copies(d):
            copy().start()

    def own_pack(d):
        for copy in inner_copies(d):
            copy().wait_recv()
        high = up8(d)
        at = d + (1 - core) * (COLS - d)
        row = lax.broadcasted_iota(jnp.int32, (d, high, BR), 1)
        z[pl.ds(BASE[d] + 2 * PLANE[d] + at, d), 0:high] += jnp.where(row < d, IU[d][...], 0.0)
        z[pl.ds(BASE[d] + at, d), ROWS - high : ROWS] += jnp.where(row >= high - d, ID[d][...], 0.0)
        pack(d, d, COLS, HU[d], HD[d])

    def inner_side(d):
        at = (1 - core) * (COLS + d)
        for k in range(0, d, 6):
            SI[d][ROWS * k : ROWS * (k + 6)] = summed(d, at + k, 6).astype(BF)
        side_copies(d)[1]().start()

    def outer_side(d):
        arrive_rows(corner_copies(d))
        at = core * (COLS + d)
        for k in range(0, d, 6):
            SO[d][ROWS * k : ROWS * (k + 6)] = summed(d, at + k, 6, (GCU, GCD), k).astype(BF)

        @pl.when(has_outer)
        def _():
            side_copies(d)[0]().start()

    def own_in(d):
        arrive_rows(own_copies(d))
        for k in range(0, COLS, 4):
            at = BASE[d] + PLANE[d] + d + k
            z[at : at + 4] = summed(d, d + k, 4, (GHU, GHD), k).reshape(4, ROWS, BR)

    def pool_first():
        for k in range(1, n_row):
            pool_row(k).start()

    def pool_second():
        for k in range(1, n_row):
            pool_row(k).wait_recv()
        acc = prow[0]
        for k in range(1, n_row):
            acc = acc + prow[k]
        pcol[0] = acc
        for k in range(1, n_col):
            pool_col(k).start()

    def pool_third():
        for k in range(1, n_col):
            pool_col(k).wait_recv()
        acc = pcol[0]
        for k in range(1, n_col):
            acc = acc + pcol[k]
        pooled = (acc / (PIX * n_row * n_col)).astype(BF).astype(F32)
        side = jnp.transpose(pooled, (1, 0))
        parts = jnp.zeros((8, BR), F32)
        for k in range(lanes):
            prod = side[:, k : k + 1] * wpool[BR * k : BR * k + BR].astype(F32)
            parts = parts + jnp.sum(prod.reshape(BR // 8, 8, BR), axis=0)
        branch = jnp.maximum(jnp.sum(parts, axis=0, keepdims=True), 0.0)
        branch = jnp.broadcast_to(branch, (16, BR)).astype(BF)
        return jnp.dot(branch, wproj[4 * BR : 5 * BR], preferred_element_type=F32)[0:1]

    filled = set()

    def put(at, y):
        y = y.reshape(COLS, ROWS, BR)
        k = 0
        while k < COLS:
            old = at + k in filled
            n = 1
            while k + n < COLS and (at + k + n in filled) == old:
                n += 1
            if old:
                z[at + k : at + k + n] += y[k : k + n]
            else:
                z[at + k : at + k + n] = y[k : k + n]
            k += n
        filled.update(range(at, at + COLS))

    def multiply(step):
        pltpu.make_async_copy(w.at[step], w.at[step], wsem.at[step]).wait()
        if step + 3 < STEPS:
            start_weights(step + 3)
        if step == 3:
            for copy in late:
                copy.start()
        taps = jnp.concatenate([w[step, k] for k in range(TAPS)], axis=1)
        half = PIX // 2
        y = jnp.concatenate(
            [jnp.dot(x[at : at + half], taps, preferred_element_type=F32) for at in (0, half)], axis=0)
        for k, tap in enumerate(taps_of(step)):
            at = POINT
            if tap is not None:
                d, a, b = tap
                at = BASE[d] + a * PLANE[d] + (2 - b) * d
            put(at, y[:, BR * k : BR * k + BR])

    hole = BASE[18] + PLANE[18] + COLS
    z[hole : hole + 36 - COLS] = jnp.zeros((36 - COLS, ROWS, BR), F32)
    filled.update(range(hole, hole + 36 - COLS))

    multiply(0)
    pl.semaphore_wait(barrier, n_row + n_col - 2)
    corners_out(18)
    pool_first()
    multiply(1)
    own_pack(18)
    inner_side(18)
    multiply(2)
    corners_out(12)
    start_rows(own_copies(18))
    outer_side(18)
    pool_second()
    multiply(3)
    own_pack(12)
    inner_side(12)
    start_rows(own_copies(12))
    multiply(4)
    corners_out(6)
    outer_side(12)
    multiply(5)
    own_pack(6)
    inner_side(6)
    outer_side(6)
    start_rows(own_copies(6))
    multiply(6)
    for copy in late:
        copy.wait()
    for d in RATES:
        own_in(d)
    pool_part = pool_third()
    joined[:, 0:BR] = jnp.maximum(z[POINT : POINT + COLS], 0.0).reshape(PIX, BR).astype(BF)

    for n, d in ((3, 18), (2, 12), (1, 6)):
        side_copies(d)[1]().wait_recv()

        @pl.when(has_outer)
        def _(d=d):
            side_copies(d)[0]().wait_recv()

        at = BASE[d] + PLANE[d] + d
        for buf, side in ((RO[d], core), (RI[d], 1 - core)):
            z[pl.ds(at + side * (COLS - d), d)] += buf[...].astype(F32).reshape(d, ROWS, BR)
        joined[:, BR * n : BR * (n + 1)] = jnp.maximum(z[at : at + COLS], 0.0).reshape(PIX, BR).astype(BF)

    for at in (0, PIX // 2):
        rows = slice(at, at + PIX // 2)
        mixed = jnp.dot(joined[rows], wproj[0 : 4 * BR], preferred_element_type=F32)
        out_ref[rows] = jnp.maximum(mixed + pool_part, 0.0).astype(BF)

    for k in range(1, n_row):
        pool_row(k).wait_send()
    for k in range(1, n_col):
        pool_col(k).wait_send()
    for d in RATES:
        inner_copies(d)[0]().wait_send()
        inner_copies(d)[1]().wait_send()
        side_copies(d)[1]().wait_send()
        for there, copy in (
            (has_up, corner_copies(d)[0]), (has_down, corner_copies(d)[1]),
            (has_up, own_copies(d)[0]), (has_down, own_copies(d)[1]), (has_outer, side_copies(d)[0]),
        ):
            @pl.when(there)
            def _(copy=copy):
                copy().wait_send()


def per_device(n_row, n_col, features, w_point, w_rate_six, w_rate_twelve, w_rate_eighteen, w_pool, w_proj):
    chans = features.shape[2]
    lanes = chans // BR
    vm = pltpu.VMEM
    dma = pltpu.SemaphoreType.DMA
    scratch = [vm((PIX, chans), BF), vm((STEPS, TAPS, chans, BR), BF), vm((chans, BR), BF), vm((5 * BR, OUT), BF)]
    scratch += [vm((POINT + COLS, ROWS, BR), F32), vm((PIX, 4 * BR), BF)]
    for size in (lambda d: up16(d * d), lambda d: up16(COLS * d), lambda d: ROWS * d):
        for _ in range(4):
            scratch += [vm((size(d), BR), BF) for d in RATES]
    for _ in range(2):
        scratch += [vm((d, up8(d), BR), F32) for d in RATES]
    scratch += [vm((n_row, lanes, BR), F32), vm((n_col, lanes, BR), F32)]
    scratch += [dma((XPARTS,)), dma((STEPS,)), dma((2,))] + [dma((6,))] * 8
    scratch += [dma((n_row,)), dma((n_row,)), dma((n_col,)), dma((n_col,))]
    pixels = jnp.transpose(features, (1, 0, 2)).reshape(PIX, chans)
    out = pl.pallas_call(
        functools.partial(body, n_row, n_col),
        name="aspp_branches",
        out_shape=jax.ShapeDtypeStruct((PIX, OUT), BF),
        in_specs=[pl.BlockSpec(memory_space=pltpu.HBM)] * 7,
        out_specs=pl.BlockSpec(memory_space=pltpu.VMEM),
        scratch_shapes=scratch,
        compiler_params=pltpu.CompilerParams(
            collective_id=0, has_side_effects=True, vmem_limit_bytes=48 << 20),
        cost_estimate=pl.CostEstimate(
            flops=2 * PIX * chans * BR * 28, bytes_accessed=20 << 20, transcendentals=0),
    )(*[pltpu.with_memory_space_constraint(a, pltpu.HBM) for a in (
        pixels, w_point, w_rate_six, w_rate_twelve, w_rate_eighteen, w_pool, w_proj)])
    return jnp.transpose(out.reshape(COLS, ROWS, OUT), (1, 0, 2))


def solution(mesh):
    placed = (P("row", "col", None), P(), P(), P(), P(), P(), P())
    return jax.shard_map(
        functools.partial(per_device, mesh.shape["row"], mesh.shape["col"]),
        mesh=mesh, in_specs=placed, out_specs=P("row", "col", None), check_vma=False)
```

```python
import functools

import jax
import jax.numpy as jnp
from jax import lax
from jax.experimental import pallas as pl
from jax.experimental.pallas import tpu as pltpu
from jax.sharding import PartitionSpec as P

MESH = pl.DeviceIdType.MESH
BF = jnp.bfloat16
F32 = jnp.float32
RATES = (18, 12, 6)
ROWS, COLS, BR, OUT = 40, 20, 128, 256
PIX = ROWS * COLS
PACK = {18: 8, 12: 4, 6: 8}
XPARTS = 2
STEPS, TAPS = 7, 4
PLANE = {d: COLS + 2 * d for d in RATES}
BASE = {18: 0, 12: 3 * PLANE[18], 6: 3 * (PLANE[18] + PLANE[12])}
POINT = 3 * (PLANE[18] + PLANE[12] + PLANE[6])


def up16(n):
    return -(-n // 16) * 16


def up8(n):
    return -(-n // 8) * 8


def take(buf, start, stop):
    low, high = start // 16 * 16, up16(stop)
    return buf[low:high].astype(F32)[start - low : stop - low]


ORDER = (
    ((18, 0, 2), (18, 2, 2), (18, 0, 0), (18, 2, 0)),
    ((18, 0, 1), (18, 2, 1), (12, 0, 2), (12, 2, 2)),
    ((18, 1, 2), (18, 1, 0), (12, 0, 0), (12, 2, 0)),
    ((6, 0, 2), (6, 2, 2), (6, 0, 0), (6, 2, 0)),
    ((12, 0, 1), (12, 2, 1), (12, 1, 2), (12, 1, 0)),
    ((6, 0, 1), (6, 2, 1), (6, 1, 2), (6, 1, 0)),
    ((18, 1, 1), (12, 1, 1), (6, 1, 1), None),
)


def body(
    n_row, n_col,
    x_hbm, wp_hbm, w6_hbm, w12_hbm, w18_hbm, wpool_hbm, wproj_hbm,
    out_ref,
    x, w, wpool, wproj, z, joined,
    cu18, cu12, cu6, cd18, cd12, cd6, gcu18, gcu12, gcu6, gcd18, gcd12, gcd6,
    hu18, hu12, hu6, hd18, hd12, hd6, ghu18, ghu12, ghu6, ghd18, ghd12, ghd6,
    so18, so12, so6, si18, si12, si6, ro18, ro12, ro6, ri18, ri12, ri6,
    iu18, iu12, iu6, id18, id12, id6,
    shares, got_shares, sums, products,
    xsem, wsem, wpsem, row_ss, row_rs, own_ss, own_rs, col_ss, col_rs, in_ss, in_rs, ps_ss, ps_rs, pc_ss, pc_rs, pp_ss, pp_rs,
):
    r = lax.axis_index("row")
    c = lax.axis_index("col")
    core = lax.rem(c, 2)
    has_up, has_down = r > 0, r < n_row - 1
    has_outer = jnp.logical_and(c > 0, c < n_col - 1)
    up, down = lax.rem(r + n_row - 1, n_row), lax.rem(r + 1, n_row)
    outer, inner = lax.rem(c + n_col - 1 + 2 * core, n_col), c + 1 - 2 * core

    by = lambda *bufs: dict(zip(RATES, bufs))
    CU, CD, GCU, GCD = by(cu18, cu12, cu6), by(cd18, cd12, cd6), by(gcu18, gcu12, gcu6), by(gcd18, gcd12, gcd6)
    HU, HD, GHU, GHD = by(hu18, hu12, hu6), by(hd18, hd12, hd6), by(ghu18, ghu12, ghu6), by(ghd18, ghd12, ghd6)
    SO, SI, RO, RI = by(so18, so12, so6), by(si18, si12, si6), by(ro18, ro12, ro6), by(ri18, ri12, ri6)
    IU, ID = by(iu18, iu12, iu6), by(id18, id12, id6)
    RATE_HBM = {18: w18_hbm, 12: w12_hbm, 6: w6_hbm}

    def start_weights(step):
        for k, tap in enumerate(ORDER[step]):
            src = wp_hbm if tap is None else RATE_HBM[tap[0]].at[tap[1], tap[2]]
            pltpu.make_async_copy(src, w.at[step, k], wsem.at[step]).start()

    start_weights(0)
    xcopies = []
    part = PIX // XPARTS
    for i in range(XPARTS):
        cp = pltpu.make_async_copy(x_hbm.at[pl.ds(part * i, part)], x.at[pl.ds(part * i, part)], xsem.at[i])
        cp.start()
        xcopies.append(cp)
    late = [pltpu.make_async_copy(wpool_hbm, wpool, wpsem.at[0]), pltpu.make_async_copy(wproj_hbm, wproj, wpsem.at[1])]

    barrier = pltpu.get_barrier_semaphore()
    for k in range(1, n_row):
        pl.semaphore_signal(barrier, inc=1, device_id=(lax.rem(r + k, n_row), c), device_id_type=MESH)
    for k in range(1, n_col):
        pl.semaphore_signal(barrier, inc=1, device_id=(r, lax.rem(c + k, n_col)), device_id_type=MESH)

    for there, bufs in ((has_up, (GCD, GHD)), (has_down, (GCU, GHU)), (has_outer, (RO,))):
        @pl.when(jnp.logical_not(there))
        def _(bufs=bufs):
            for buf in bufs:
                for d in RATES:
                    buf[d][...] = jnp.zeros_like(buf[d])

    chans = x.shape[1]
    lanes = chans // BR
    share = chans // n_row

    def remote(src, dst, sems, n, to):
        return pltpu.make_async_remote_copy(
            src_ref=src, dst_ref=dst, send_sem=sems[0].at[n], recv_sem=sems[1].at[n],
            device_id=to, device_id_type=MESH)

    def share_copy(k):
        to = lax.rem(r + k, n_row)
        return remote(shares.at[to], got_shares.at[k], (ps_ss, ps_rs), k, (to, c))

    def sum_copy(k):
        return remote(sums.at[0], sums.at[k], (pc_ss, pc_rs), k, (r, lax.rem(c + k, n_col)))

    def product_copy(k):
        return remote(products.at[0], products.at[k], (pp_ss, pp_rs), k, (lax.rem(r + k, n_row), c))

    def corner_copies(d):
        n = 2 * RATES.index(d)
        return (lambda: remote(CU[d], GCU[d], (row_ss, row_rs), n, (up, c)),
                lambda: remote(CD[d], GCD[d], (row_ss, row_rs), n + 1, (down, c)))

    def own_copies(d):
        n = 2 * RATES.index(d)
        return (lambda: remote(HU[d], GHU[d], (own_ss, own_rs), n, (up, c)),
                lambda: remote(HD[d], GHD[d], (own_ss, own_rs), n + 1, (down, c)))

    def side_copies(d):
        n = 2 * RATES.index(d)
        return (lambda: remote(SO[d], RO[d], (col_ss, col_rs), n, (r, outer)),
                lambda: remote(SI[d], RI[d], (col_ss, col_rs), n + 1, (r, inner)))

    def inner_copies(d):
        n = 2 * RATES.index(d)
        high = up8(d)
        at = (1 - core) * (COLS + d)
        src_u = z.at[pl.ds(BASE[d] + 2 * PLANE[d] + at, d), pl.ds(0, high)]
        src_d = z.at[pl.ds(BASE[d] + at, d), pl.ds(ROWS - high, high)]
        return (lambda: remote(src_u, IU[d], (in_ss, in_rs), n, (r, inner)),
                lambda: remote(src_d, ID[d], (in_ss, in_rs), n + 1, (r, inner)))

    def start_rows(copies):
        @pl.when(has_up)
        def _():
            copies[0]().start()

        @pl.when(has_down)
        def _():
            copies[1]().start()

    def arrive_rows(copies):
        @pl.when(has_down)
        def _():
            copies[0]().wait_recv()

        @pl.when(has_up)
        def _():
            copies[1]().wait_recv()

    def pack(d, at, count, to_up, to_down):
        g = PACK[d]
        for k in range(0, count, g):
            n = min(g, count - k)
            gap = [jnp.zeros((up16(n * d) - n * d, BR), F32)] if n * d % 16 else []
            rows = slice(k * d, k * d + up16(n * d))
            tops = [z[BASE[d] + 2 * PLANE[d] + at + k + j][0:d] for j in range(n)]
            ends = [z[BASE[d] + at + k + j][ROWS - d : ROWS] for j in range(n)]
            to_up[rows] = jnp.concatenate(tops + gap, axis=0).astype(BF)
            to_down[rows] = jnp.concatenate(ends + gap, axis=0).astype(BF)

    def summed(d, at, count, got=None, k=0):
        if got is None:
            got_u = got_d = jnp.zeros((count * d, BR), F32)
        else:
            got_u, got_d = (take(buf[d], k * d, (k + count) * d) for buf in got)
        above, below, same = [], [], []
        for j in range(count):
            z0, z1, z2 = (z[BASE[d] + a * PLANE[d] + at + j] for a in range(3))
            above += [got_d[j * d : (j + 1) * d], z0[0 : ROWS - d]]
            below += [z2[d:ROWS], got_u[j * d : (j + 1) * d]]
            same.append(z1)
        return sum(jnp.concatenate(parts, axis=0) for parts in (same, above, below))

    def corners_out(d):
        pack(d, core * (COLS + d), d, CU[d], CD[d])
        start_rows(corner_copies(d))
        for copy in inner_copies(d):
            copy().start()

    def own_arrive(d):
        for copy in inner_copies(d):
            copy().wait_recv()

    def own_pack(d):
        high = up8(d)
        at = d + (1 - core) * (COLS - d)
        row = lax.broadcasted_iota(jnp.int32, (d, high, BR), 1)
        z[pl.ds(BASE[d] + 2 * PLANE[d] + at, d), 0:high] += jnp.where(row < d, IU[d][...], 0.0)
        z[pl.ds(BASE[d] + at, d), ROWS - high : ROWS] += jnp.where(row >= high - d, ID[d][...], 0.0)
        pack(d, d, COLS, HU[d], HD[d])

    def inner_side(d):
        at = (1 - core) * (COLS + d)
        for k in range(0, d, 6):
            SI[d][ROWS * k : ROWS * (k + 6)] = summed(d, at + k, 6).astype(BF)
        side_copies(d)[1]().start()

    def outer_side(d):
        at = core * (COLS + d)
        for k in range(0, d, 6):
            SO[d][ROWS * k : ROWS * (k + 6)] = summed(d, at + k, 6, (GCU, GCD), k).astype(BF)

        @pl.when(has_outer)
        def _():
            side_copies(d)[0]().start()

    def own_in(d):
        for k in range(0, COLS, 4):
            at = BASE[d] + PLANE[d] + d + k
            z[at : at + 4] = summed(d, d + k, 4, (GHU, GHD), k).reshape(4, ROWS, BR)

    def pixel_sum():
        for k in range(lanes):
            acc = jnp.zeros((8, BR), F32)
            for at in range(0, PIX, 16):
                rows = x[at : at + 16, BR * k : BR * k + BR].astype(F32)
                acc = acc + (rows[0:8] + rows[8:16])
            n, at = divmod(BR * k, share)
            shares[n, :, at : at + BR] = jnp.sum(acc, axis=0, keepdims=True)

    def pool_first():
        for k in range(1, n_row):
            share_copy(k).start()

    def pool_second():
        for k in range(1, n_row):
            share_copy(k).wait_recv()
        acc = shares[r]
        for k in range(1, n_row):
            acc = acc + got_shares[k]
        sums[0] = acc
        for k in range(1, n_col):
            sum_copy(k).start()

    def pool_third():
        for k in range(1, n_col):
            sum_copy(k).wait_recv()
        acc = sums[0]
        for k in range(1, n_col):
            acc = acc + sums[k]
        pooled = (acc / (PIX * n_row * n_col)).astype(BF).astype(F32)
        parts = jnp.zeros((8, BR), F32)
        for k in range(share // BR):
            side = jnp.transpose(jnp.broadcast_to(pooled[:, BR * k : BR * k + BR], (8, BR)), (1, 0))[:, 0:1]
            rows = wpool[pl.ds(pl.multiple_of(r * share + BR * k, BR), BR)]
            parts = parts + jnp.sum((side * rows.astype(F32)).reshape(BR // 8, 8, BR), axis=0)
        products[0] = jnp.sum(parts, axis=0, keepdims=True)
        for k in range(1, n_row):
            product_copy(k).start()

    def pool_fourth():
        for k in range(1, n_row):
            product_copy(k).wait_recv()
        acc = products[0]
        for k in range(1, n_row):
            acc = acc + products[k]
        branch = jnp.broadcast_to(jnp.maximum(acc, 0.0), (16, BR)).astype(BF)
        return jnp.dot(branch, wproj[4 * BR : 5 * BR], preferred_element_type=F32)[0:1]

    filled = set()

    def put(at, y):
        cols = y.shape[0] // ROWS
        y = y.reshape(cols, ROWS, BR)
        k = 0
        while k < cols:
            old = at + k in filled
            n = 1
            while k + n < cols and (at + k + n in filled) == old:
                n += 1
            if old:
                z[at + k : at + k + n] += y[k : k + n]
            else:
                z[at + k : at + k + n] = y[k : k + n]
            k += n
        filled.update(range(at, at + cols))

    def weights_in(step):
        pltpu.make_async_copy(w.at[step], w.at[step], wsem.at[step]).wait()
        if 0 < step < STEPS - 2:
            start_weights(step + 2)
        if step == 2:
            for copy in late:
                copy.start()

    def multiply(step, first=None):
        taps = jnp.concatenate([w[step, k] for k in range(TAPS)], axis=1)
        half = PIX // 2
        if first is None:
            y = jnp.concatenate(
                [jnp.dot(x[at : at + half], taps, preferred_element_type=F32) for at in (0, half)], axis=0)
        else:
            y = jnp.dot(x[first : first + half], taps, preferred_element_type=F32)
        for k, tap in enumerate(ORDER[step]):
            at = POINT
            if tap is not None:
                d, a, b = tap
                at = BASE[d] + a * PLANE[d] + (2 - b) * d
            put(at + (first or 0) // ROWS, y[:, BR * k : BR * k + BR])

    hole = BASE[18] + PLANE[18] + COLS
    z[hole : hole + 36 - COLS] = jnp.zeros((36 - COLS, ROWS, BR), F32)
    filled.update(range(hole, hole + 36 - COLS))

    xcopies[0].wait()
    weights_in(0)
    start_weights(1)
    multiply(0, 0)
    xcopies[1].wait()
    start_weights(2)
    pixel_sum()
    multiply(0, PIX // 2)
    pl.semaphore_wait(barrier, n_row + n_col - 2)
    weights_in(1)
    pool_first()
    corners_out(18)
    multiply(1)
    own_arrive(18)
    weights_in(2)
    own_pack(18)
    start_rows(own_copies(18))
    multiply(2)
    pool_second()
    arrive_rows(corner_copies(18))
    weights_in(3)
    corners_out(12)
    outer_side(18)
    inner_side(18)
    multiply(3)
    weights_in(4)
    corners_out(6)
    multiply(4)
    for copy in late:
        copy.wait()
    pool_third()
    own_arrive(12)
    arrive_rows(corner_copies(12))
    weights_in(5)
    outer_side(12)
    own_pack(12)
    start_rows(own_copies(12))
    inner_side(12)
    arrive_rows(own_copies(18))
    own_in(18)
    multiply(5)
    own_arrive(6)
    arrive_rows(corner_copies(6))
    weights_in(6)
    own_pack(6)
    start_rows(own_copies(6))
    outer_side(6)
    inner_side(6)
    multiply(6)
    arrive_rows(own_copies(12))
    own_in(12)
    arrive_rows(own_copies(6))
    own_in(6)
    pool_part = pool_fourth()
    joined[:, 0:BR] = jnp.maximum(z[POINT : POINT + COLS], 0.0).reshape(PIX, BR).astype(BF)

    for n, d in ((3, 18), (2, 12), (1, 6)):
        side_copies(d)[1]().wait_recv()

        @pl.when(has_outer)
        def _(d=d):
            side_copies(d)[0]().wait_recv()

        at = BASE[d] + PLANE[d] + d
        for buf, side in ((RO[d], core), (RI[d], 1 - core)):
            z[pl.ds(at + side * (COLS - d), d)] += buf[...].astype(F32).reshape(d, ROWS, BR)
        joined[:, BR * n : BR * (n + 1)] = jnp.maximum(z[at : at + COLS], 0.0).reshape(PIX, BR).astype(BF)

    for at in (0, PIX // 2):
        rows = slice(at, at + PIX // 2)
        mixed = jnp.dot(joined[rows], wproj[0 : 4 * BR], preferred_element_type=F32)
        out_ref[rows] = jnp.maximum(mixed + pool_part, 0.0).astype(BF)

    for k in range(1, n_row):
        share_copy(k).wait_send()
        product_copy(k).wait_send()
    for k in range(1, n_col):
        sum_copy(k).wait_send()
    for d in RATES:
        inner_copies(d)[0]().wait_send()
        inner_copies(d)[1]().wait_send()
        side_copies(d)[1]().wait_send()
        for there, copy in (
            (has_up, corner_copies(d)[0]), (has_down, corner_copies(d)[1]),
            (has_up, own_copies(d)[0]), (has_down, own_copies(d)[1]), (has_outer, side_copies(d)[0]),
        ):
            @pl.when(there)
            def _(copy=copy):
                copy().wait_send()


def per_device(n_row, n_col, features, w_point, w_rate_six, w_rate_twelve, w_rate_eighteen, w_pool, w_proj):
    chans = features.shape[2]
    vm = pltpu.VMEM
    dma = pltpu.SemaphoreType.DMA
    scratch = [vm((PIX, chans), BF), vm((STEPS, TAPS, chans, BR), BF), vm((chans, BR), BF), vm((5 * BR, OUT), BF)]
    scratch += [vm((POINT + COLS, ROWS, BR), F32), vm((PIX, 4 * BR), BF)]
    for size in (lambda d: up16(d * d), lambda d: up16(COLS * d), lambda d: ROWS * d):
        for _ in range(4):
            scratch += [vm((size(d), BR), BF) for d in RATES]
    for _ in range(2):
        scratch += [vm((d, up8(d), BR), F32) for d in RATES]
    share = chans // n_row
    scratch += [vm((n_row, 1, share), F32), vm((n_row, 1, share), F32), vm((n_col, 1, share), F32), vm((n_row, 1, BR), F32)]
    scratch += [dma((XPARTS,)), dma((STEPS,)), dma((2,))] + [dma((6,))] * 8
    scratch += [dma((n_row,)), dma((n_row,)), dma((n_col,)), dma((n_col,)), dma((n_row,)), dma((n_row,))]
    pixels = jnp.transpose(features, (1, 0, 2)).reshape(PIX, chans)
    out = pl.pallas_call(
        functools.partial(body, n_row, n_col),
        name="aspp_branches",
        out_shape=jax.ShapeDtypeStruct((PIX, OUT), BF),
        in_specs=[pl.BlockSpec(memory_space=pltpu.HBM)] * 7,
        out_specs=pl.BlockSpec(memory_space=pltpu.VMEM),
        scratch_shapes=scratch,
        compiler_params=pltpu.CompilerParams(
            collective_id=0, has_side_effects=True, vmem_limit_bytes=48 << 20),
        cost_estimate=pl.CostEstimate(
            flops=2 * PIX * chans * BR * 28, bytes_accessed=20 << 20, transcendentals=0),
    )(*[pltpu.with_memory_space_constraint(a, pltpu.HBM) for a in (
        pixels, w_point, w_rate_six, w_rate_twelve, w_rate_eighteen, w_pool, w_proj)])
    return jnp.transpose(out.reshape(COLS, ROWS, OUT), (1, 0, 2))


def solution(mesh):
    placed = (P("row", "col", None), P(), P(), P(), P(), P(), P())
    return jax.shard_map(
        functools.partial(per_device, mesh.shape["row"], mesh.shape["col"]),
        mesh=mesh, in_specs=placed, out_specs=P("row", "col", None), check_vma=False)
```

```python
import functools

import jax
import jax.numpy as jnp
from jax import lax
from jax.experimental import pallas as pl
from jax.experimental.pallas import tpu as pltpu
from jax.sharding import PartitionSpec as P

MESH = pl.DeviceIdType.MESH
BF = jnp.bfloat16
F32 = jnp.float32
RATES = (18, 12, 6)
ROWS, COLS, BR, OUT = 40, 20, 128, 256
PIX = ROWS * COLS
PACK = {18: 8, 12: 4, 6: 8}
XPARTS = 2
STEPS, TAPS = 7, 4
PLANE = {d: COLS + 2 * d for d in RATES}
BASE = {18: 0, 12: 3 * PLANE[18], 6: 3 * (PLANE[18] + PLANE[12])}
POINT = 3 * (PLANE[18] + PLANE[12] + PLANE[6])


def up16(n):
    return -(-n // 16) * 16


def up8(n):
    return -(-n // 8) * 8


def take(buf, start, stop):
    low, high = start // 16 * 16, up16(stop)
    return buf[low:high].astype(F32)[start - low : stop - low]


ORDER = (
    ((18, 0, 2), (18, 2, 2), (18, 0, 0), (18, 2, 0)),
    ((18, 0, 1), (18, 2, 1), (12, 0, 2), (12, 2, 2)),
    ((18, 1, 2), (18, 1, 0), (12, 0, 0), (12, 2, 0)),
    ((6, 0, 2), (6, 2, 2), (6, 0, 0), (6, 2, 0)),
    ((12, 0, 1), (12, 2, 1), (12, 1, 2), (12, 1, 0)),
    ((6, 0, 1), (6, 2, 1), (6, 1, 2), (6, 1, 0)),
    ((18, 1, 1), (12, 1, 1), (6, 1, 1), None),
)


def body(
    n_row, n_col,
    x_hbm, wp_hbm, w6_hbm, w12_hbm, w18_hbm, wpool_hbm, wproj_hbm,
    out_ref,
    x, w, wpool, wproj, z, joined,
    cu18, cu12, cu6, cd18, cd12, cd6, gcu18, gcu12, gcu6, gcd18, gcd12, gcd6,
    hu18, hu12, hu6, hd18, hd12, hd6, ghu18, ghu12, ghu6, ghd18, ghd12, ghd6,
    so18, so12, so6, si18, si12, si6, ro18, ro12, ro6, ri18, ri12, ri6,
    iu18, iu12, iu6, id18, id12, id6,
    shares, got_shares, sums, products,
    xsem, wsem, wpsem, row_ss, row_rs, own_ss, own_rs, col_ss, col_rs, in_ss, in_rs, ps_ss, ps_rs, pc_ss, pc_rs, pp_ss, pp_rs,
):
    r = lax.axis_index("row")
    c = lax.axis_index("col")
    core = lax.rem(c, 2)
    has_up, has_down = r > 0, r < n_row - 1
    has_outer = jnp.logical_and(c > 0, c < n_col - 1)
    up, down = lax.rem(r + n_row - 1, n_row), lax.rem(r + 1, n_row)
    outer, inner = lax.rem(c + n_col - 1 + 2 * core, n_col), c + 1 - 2 * core

    by = lambda *bufs: dict(zip(RATES, bufs))
    CU, CD, GCU, GCD = by(cu18, cu12, cu6), by(cd18, cd12, cd6), by(gcu18, gcu12, gcu6), by(gcd18, gcd12, gcd6)
    HU, HD, GHU, GHD = by(hu18, hu12, hu6), by(hd18, hd12, hd6), by(ghu18, ghu12, ghu6), by(ghd18, ghd12, ghd6)
    SO, SI, RO, RI = by(so18, so12, so6), by(si18, si12, si6), by(ro18, ro12, ro6), by(ri18, ri12, ri6)
    IU, ID = by(iu18, iu12, iu6), by(id18, id12, id6)
    RATE_HBM = {18: w18_hbm, 12: w12_hbm, 6: w6_hbm}

    def start_weights(step):
        for k, tap in enumerate(ORDER[step]):
            src = wp_hbm if tap is None else RATE_HBM[tap[0]].at[tap[1], tap[2]]
            pltpu.make_async_copy(src, w.at[step, k], wsem.at[step]).start()

    start_weights(0)
    xcopies = []
    part = PIX // XPARTS
    for i in range(XPARTS):
        cp = pltpu.make_async_copy(x_hbm.at[pl.ds(part * i, part)], x.at[pl.ds(part * i, part)], xsem.at[i])
        cp.start()
        xcopies.append(cp)
    late = [pltpu.make_async_copy(wpool_hbm, wpool, wpsem.at[0]), pltpu.make_async_copy(wproj_hbm, wproj, wpsem.at[1])]

    barrier = pltpu.get_barrier_semaphore()
    for k in range(1, n_row):
        pl.semaphore_signal(barrier, inc=1, device_id=(lax.rem(r + k, n_row), c), device_id_type=MESH)
    for k in range(1, n_col):
        pl.semaphore_signal(barrier, inc=1, device_id=(r, lax.rem(c + k, n_col)), device_id_type=MESH)

    for there, bufs in ((has_up, (GCD, GHD)), (has_down, (GCU, GHU)), (has_outer, (RO,))):
        @pl.when(jnp.logical_not(there))
        def _(bufs=bufs):
            for buf in bufs:
                for d in RATES:
                    buf[d][...] = jnp.zeros_like(buf[d])

    chans = x.shape[1]
    lanes = chans // BR
    share = chans // n_row

    def remote(src, dst, sems, n, to):
        return pltpu.make_async_remote_copy(
            src_ref=src, dst_ref=dst, send_sem=sems[0].at[n], recv_sem=sems[1].at[n],
            device_id=to, device_id_type=MESH)

    def share_copy(k):
        to = lax.rem(r + k, n_row)
        return remote(shares.at[to], got_shares.at[k], (ps_ss, ps_rs), k, (to, c))

    def sum_copy(k):
        return remote(sums.at[0], sums.at[k], (pc_ss, pc_rs), k, (r, lax.rem(c + k, n_col)))

    def product_copy(k):
        return remote(products.at[0], products.at[k], (pp_ss, pp_rs), k, (lax.rem(r + k, n_row), c))

    def corner_copies(d):
        n = 2 * RATES.index(d)
        return (lambda: remote(CU[d], GCU[d], (row_ss, row_rs), n, (up, c)),
                lambda: remote(CD[d], GCD[d], (row_ss, row_rs), n + 1, (down, c)))

    def own_copies(d):
        n = 2 * RATES.index(d)
        return (lambda: remote(HU[d], GHU[d], (own_ss, own_rs), n, (up, c)),
                lambda: remote(HD[d], GHD[d], (own_ss, own_rs), n + 1, (down, c)))

    def side_copies(d):
        n = 2 * RATES.index(d)
        return (lambda: remote(SO[d], RO[d], (col_ss, col_rs), n, (r, outer)),
                lambda: remote(SI[d], RI[d], (col_ss, col_rs), n + 1, (r, inner)))

    def inner_copies(d):
        n = 2 * RATES.index(d)
        high = up8(d)
        at = (1 - core) * (COLS + d)
        src_u = z.at[pl.ds(BASE[d] + 2 * PLANE[d] + at, d), pl.ds(0, high)]
        src_d = z.at[pl.ds(BASE[d] + at, d), pl.ds(ROWS - high, high)]
        return (lambda: remote(src_u, IU[d], (in_ss, in_rs), n, (r, inner)),
                lambda: remote(src_d, ID[d], (in_ss, in_rs), n + 1, (r, inner)))

    def start_rows(copies):
        @pl.when(has_up)
        def _():
            copies[0]().start()

        @pl.when(has_down)
        def _():
            copies[1]().start()

    def arrive_rows(copies):
        @pl.when(has_down)
        def _():
            copies[0]().wait_recv()

        @pl.when(has_up)
        def _():
            copies[1]().wait_recv()

    def pack(d, at, count, to_up, to_down):
        g = PACK[d]
        for k in range(0, count, g):
            n = min(g, count - k)
            gap = [jnp.zeros((up16(n * d) - n * d, BR), F32)] if n * d % 16 else []
            rows = slice(k * d, k * d + up16(n * d))
            tops = [z[BASE[d] + 2 * PLANE[d] + at + k + j][0:d] for j in range(n)]
            ends = [z[BASE[d] + at + k + j][ROWS - d : ROWS] for j in range(n)]
            to_up[rows] = jnp.concatenate(tops + gap, axis=0).astype(BF)
            to_down[rows] = jnp.concatenate(ends + gap, axis=0).astype(BF)

    def summed(d, at, count, got=None, k=0):
        if got is None:
            got_u = got_d = jnp.zeros((count * d, BR), F32)
        else:
            got_u, got_d = (take(buf[d], k * d, (k + count) * d) for buf in got)
        above, below, same = [], [], []
        for j in range(count):
            z0, z1, z2 = (z[BASE[d] + a * PLANE[d] + at + j] for a in range(3))
            above += [got_d[j * d : (j + 1) * d], z0[0 : ROWS - d]]
            below += [z2[d:ROWS], got_u[j * d : (j + 1) * d]]
            same.append(z1)
        return sum(jnp.concatenate(parts, axis=0) for parts in (same, above, below))

    def corners_out(d):
        pack(d, core * (COLS + d), d, CU[d], CD[d])
        start_rows(corner_copies(d))
        for copy in inner_copies(d):
            copy().start()

    def own_arrive(d):
        for copy in inner_copies(d):
            copy().wait_recv()

    def own_pack(d):
        high = up8(d)
        at = d + (1 - core) * (COLS - d)
        row = lax.broadcasted_iota(jnp.int32, (d, high, BR), 1)
        z[pl.ds(BASE[d] + 2 * PLANE[d] + at, d), 0:high] += jnp.where(row < d, IU[d][...], 0.0)
        z[pl.ds(BASE[d] + at, d), ROWS - high : ROWS] += jnp.where(row >= high - d, ID[d][...], 0.0)
        pack(d, d, COLS, HU[d], HD[d])

    def inner_side(d):
        at = (1 - core) * (COLS + d)
        for k in range(0, d, 6):
            SI[d][ROWS * k : ROWS * (k + 6)] = summed(d, at + k, 6).astype(BF)
        side_copies(d)[1]().start()

    def outer_side(d):
        at = core * (COLS + d)
        for k in range(0, d, 6):
            SO[d][ROWS * k : ROWS * (k + 6)] = summed(d, at + k, 6, (GCU, GCD), k).astype(BF)

        @pl.when(has_outer)
        def _():
            side_copies(d)[0]().start()

    def own_in(d):
        for k in range(0, COLS, 4):
            at = BASE[d] + PLANE[d] + d + k
            z[at : at + 4] = summed(d, d + k, 4, (GHU, GHD), k).reshape(4, ROWS, BR)

    def pixel_sum():
        for k in range(lanes):
            acc = jnp.zeros((8, BR), F32)
            for at in range(0, PIX, 16):
                rows = x[at : at + 16, BR * k : BR * k + BR].astype(F32)
                acc = acc + (rows[0:8] + rows[8:16])
            n, at = divmod(BR * k, share)
            shares[n, :, at : at + BR] = jnp.sum(acc, axis=0, keepdims=True)

    def pool_first():
        for k in range(1, n_row):
            share_copy(k).start()

    def pool_second():
        for k in range(1, n_row):
            share_copy(k).wait_recv()
        acc = shares[r]
        for k in range(1, n_row):
            acc = acc + got_shares[k]
        sums[0] = acc
        for k in range(1, n_col):
            sum_copy(k).start()

    def pool_third():
        for k in range(1, n_col):
            sum_copy(k).wait_recv()
        acc = sums[0]
        for k in range(1, n_col):
            acc = acc + sums[k]
        pooled = (acc / (PIX * n_row * n_col)).astype(BF).astype(F32)
        parts = jnp.zeros((8, BR), F32)
        for k in range(share // BR):
            side = jnp.transpose(jnp.broadcast_to(pooled[:, BR * k : BR * k + BR], (8, BR)), (1, 0))[:, 0:1]
            rows = wpool[pl.ds(pl.multiple_of(r * share + BR * k, BR), BR)]
            parts = parts + jnp.sum((side * rows.astype(F32)).reshape(BR // 8, 8, BR), axis=0)
        products[0] = jnp.sum(parts, axis=0, keepdims=True)
        for k in range(1, n_row):
            product_copy(k).start()

    def pool_fourth():
        for k in range(1, n_row):
            product_copy(k).wait_recv()
        acc = products[0]
        for k in range(1, n_row):
            acc = acc + products[k]
        branch = jnp.broadcast_to(jnp.maximum(acc, 0.0), (16, BR)).astype(BF)
        return jnp.dot(branch, wproj[4 * BR : 5 * BR], preferred_element_type=F32)[0:1]

    filled = set()

    def put(at, y):
        cols = y.shape[0] // ROWS
        y = y.reshape(cols, ROWS, BR)
        k = 0
        while k < cols:
            old = at + k in filled
            n = 1
            while k + n < cols and (at + k + n in filled) == old:
                n += 1
            if old:
                z[at + k : at + k + n] += y[k : k + n]
            else:
                z[at + k : at + k + n] = y[k : k + n]
            k += n
        filled.update(range(at, at + cols))

    def weights_in(step):
        pltpu.make_async_copy(w.at[step], w.at[step], wsem.at[step]).wait()
        if 0 < step < STEPS - 2:
            start_weights(step + 2)
        if step == 2:
            for copy in late:
                copy.start()

    def multiply(step, first=None):
        taps = jnp.concatenate([w[step, k] for k in range(TAPS)], axis=1)
        half = PIX // 2
        if first is None:
            y = jnp.concatenate(
                [jnp.dot(x[at : at + half], taps, preferred_element_type=F32) for at in (0, half)], axis=0)
        else:
            y = jnp.dot(x[first : first + half], taps, preferred_element_type=F32)
        for k, tap in enumerate(ORDER[step]):
            at = POINT
            if tap is not None:
                d, a, b = tap
                at = BASE[d] + a * PLANE[d] + (2 - b) * d
            put(at + (first or 0) // ROWS, y[:, BR * k : BR * k + BR])

    hole = BASE[18] + PLANE[18] + COLS
    z[hole : hole + 36 - COLS] = jnp.zeros((36 - COLS, ROWS, BR), F32)
    filled.update(range(hole, hole + 36 - COLS))

    xcopies[0].wait()
    weights_in(0)
    start_weights(1)
    multiply(0, 0)
    xcopies[1].wait()
    start_weights(2)
    pixel_sum()
    multiply(0, PIX // 2)
    pl.semaphore_wait(barrier, n_row + n_col - 2)
    weights_in(1)
    pool_first()
    corners_out(18)
    multiply(1)
    own_arrive(18)
    weights_in(2)
    own_pack(18)
    start_rows(own_copies(18))
    multiply(2)
    pool_second()
    arrive_rows(corner_copies(18))
    weights_in(3)
    weights_in(4)
    corners_out(12)
    outer_side(18)
    inner_side(18)
    multiply(3)
    corners_out(6)
    multiply(4)
    own_arrive(12)
    arrive_rows(corner_copies(12))
    weights_in(5)
    outer_side(12)
    own_pack(12)
    start_rows(own_copies(12))
    inner_side(12)
    arrive_rows(own_copies(18))
    own_in(18)
    multiply(5)
    for copy in late:
        copy.wait()
    pool_third()
    own_arrive(6)
    arrive_rows(corner_copies(6))
    weights_in(6)
    own_pack(6)
    start_rows(own_copies(6))
    outer_side(6)
    inner_side(6)
    multiply(6)
    arrive_rows(own_copies(12))
    own_in(12)
    arrive_rows(own_copies(6))
    own_in(6)
    pool_part = pool_fourth()
    joined[:, 0:BR] = jnp.maximum(z[POINT : POINT + COLS], 0.0).reshape(PIX, BR).astype(BF)

    for n, d in ((3, 18), (2, 12), (1, 6)):
        side_copies(d)[1]().wait_recv()

        @pl.when(has_outer)
        def _(d=d):
            side_copies(d)[0]().wait_recv()

        at = BASE[d] + PLANE[d] + d
        for buf, side in ((RO[d], core), (RI[d], 1 - core)):
            z[pl.ds(at + side * (COLS - d), d)] += buf[...].astype(F32).reshape(d, ROWS, BR)
        joined[:, BR * n : BR * (n + 1)] = jnp.maximum(z[at : at + COLS], 0.0).reshape(PIX, BR).astype(BF)

    for at in (0, PIX // 2):
        rows = slice(at, at + PIX // 2)
        mixed = jnp.dot(joined[rows], wproj[0 : 4 * BR], preferred_element_type=F32)
        out_ref[rows] = jnp.maximum(mixed + pool_part, 0.0).astype(BF)

    for k in range(1, n_row):
        share_copy(k).wait_send()
        product_copy(k).wait_send()
    for k in range(1, n_col):
        sum_copy(k).wait_send()
    for d in RATES:
        inner_copies(d)[0]().wait_send()
        inner_copies(d)[1]().wait_send()
        side_copies(d)[1]().wait_send()
        for there, copy in (
            (has_up, corner_copies(d)[0]), (has_down, corner_copies(d)[1]),
            (has_up, own_copies(d)[0]), (has_down, own_copies(d)[1]), (has_outer, side_copies(d)[0]),
        ):
            @pl.when(there)
            def _(copy=copy):
                copy().wait_send()


def per_device(n_row, n_col, features, w_point, w_rate_six, w_rate_twelve, w_rate_eighteen, w_pool, w_proj):
    chans = features.shape[2]
    vm = pltpu.VMEM
    dma = pltpu.SemaphoreType.DMA
    scratch = [vm((PIX, chans), BF), vm((STEPS, TAPS, chans, BR), BF), vm((chans, BR), BF), vm((5 * BR, OUT), BF)]
    scratch += [vm((POINT + COLS, ROWS, BR), F32), vm((PIX, 4 * BR), BF)]
    for size in (lambda d: up16(d * d), lambda d: up16(COLS * d), lambda d: ROWS * d):
        for _ in range(4):
            scratch += [vm((size(d), BR), BF) for d in RATES]
    for _ in range(2):
        scratch += [vm((d, up8(d), BR), F32) for d in RATES]
    share = chans // n_row
    scratch += [vm((n_row, 1, share), F32), vm((n_row, 1, share), F32), vm((n_col, 1, share), F32), vm((n_row, 1, BR), F32)]
    scratch += [dma((XPARTS,)), dma((STEPS,)), dma((2,))] + [dma((6,))] * 8
    scratch += [dma((n_row,)), dma((n_row,)), dma((n_col,)), dma((n_col,)), dma((n_row,)), dma((n_row,))]
    pixels = jnp.transpose(features, (1, 0, 2)).reshape(PIX, chans)
    out = pl.pallas_call(
        functools.partial(body, n_row, n_col),
        name="aspp_branches",
        out_shape=jax.ShapeDtypeStruct((PIX, OUT), BF),
        in_specs=[pl.BlockSpec(memory_space=pltpu.HBM)] * 7,
        out_specs=pl.BlockSpec(memory_space=pltpu.VMEM),
        scratch_shapes=scratch,
        compiler_params=pltpu.CompilerParams(
            collective_id=0, has_side_effects=True, vmem_limit_bytes=48 << 20),
        cost_estimate=pl.CostEstimate(
            flops=2 * PIX * chans * BR * 28, bytes_accessed=20 << 20, transcendentals=0),
    )(*[pltpu.with_memory_space_constraint(a, pltpu.HBM) for a in (
        pixels, w_point, w_rate_six, w_rate_twelve, w_rate_eighteen, w_pool, w_proj)])
    return jnp.transpose(out.reshape(COLS, ROWS, OUT), (1, 0, 2))


def solution(mesh):
    placed = (P("row", "col", None), P(), P(), P(), P(), P(), P())
    return jax.shard_map(
        functools.partial(per_device, mesh.shape["row"], mesh.shape["col"]),
        mesh=mesh, in_specs=placed, out_specs=P("row", "col", None), check_vma=False)
```

```python
import functools

import jax
import jax.numpy as jnp
from jax import lax
from jax.experimental import pallas as pl
from jax.experimental.pallas import tpu as pltpu
from jax.sharding import PartitionSpec as P

MESH = pl.DeviceIdType.MESH
BF = jnp.bfloat16
F32 = jnp.float32
RATES = (18, 12, 6)
ROWS, COLS, BR, OUT = 40, 20, 128, 256
PIX = ROWS * COLS
PACK = {18: 8, 12: 4, 6: 8}
XPARTS = 2
STEPS, TAPS = 7, 4
PLANE = {d: COLS + 2 * d for d in RATES}
BASE = {18: 0, 12: 3 * PLANE[18], 6: 3 * (PLANE[18] + PLANE[12])}
POINT = 3 * (PLANE[18] + PLANE[12] + PLANE[6])


def up16(n):
    return -(-n // 16) * 16


def up8(n):
    return -(-n // 8) * 8


def take(buf, start, stop):
    low, high = start // 16 * 16, up16(stop)
    return buf[low:high].astype(F32)[start - low : stop - low]


ORDER = (
    ((18, 0, 2), (18, 2, 2), (18, 0, 0), (18, 2, 0)),
    ((18, 0, 1), (18, 2, 1), (12, 0, 2), (12, 2, 2)),
    ((18, 1, 2), (18, 1, 0), (12, 0, 0), (12, 2, 0)),
    ((6, 0, 2), (6, 2, 2), (6, 0, 0), (6, 2, 0)),
    ((12, 0, 1), (12, 2, 1), (12, 1, 2), (12, 1, 0)),
    ((6, 0, 1), (6, 2, 1), (6, 1, 2), (6, 1, 0)),
    ((18, 1, 1), (12, 1, 1), (6, 1, 1), None),
)


def body(
    n_row, n_col,
    x_hbm, wp_hbm, w6_hbm, w12_hbm, w18_hbm, wpool_hbm, wproj_hbm,
    out_ref,
    x, w, wpool, wproj, z, joined,
    cu18, cu12, cu6, cd18, cd12, cd6, gcu18, gcu12, gcu6, gcd18, gcd12, gcd6,
    hu18, hu12, hu6, hd18, hd12, hd6, ghu18, ghu12, ghu6, ghd18, ghd12, ghd6,
    so18, so12, so6, si18, si12, si6, ro18, ro12, ro6, ri18, ri12, ri6,
    iu18, iu12, iu6, id18, id12, id6,
    shares, got_shares, sums, products,
    xsem, wsem, wpsem, row_ss, row_rs, own_ss, own_rs, col_ss, col_rs, in_ss, in_rs, ps_ss, ps_rs, pc_ss, pc_rs, pp_ss, pp_rs,
):
    r = lax.axis_index("row")
    c = lax.axis_index("col")
    core = lax.rem(c, 2)
    has_up, has_down = r > 0, r < n_row - 1
    has_outer = jnp.logical_and(c > 0, c < n_col - 1)
    up, down = lax.rem(r + n_row - 1, n_row), lax.rem(r + 1, n_row)
    outer, inner = lax.rem(c + n_col - 1 + 2 * core, n_col), c + 1 - 2 * core

    by = lambda *bufs: dict(zip(RATES, bufs))
    CU, CD, GCU, GCD = by(cu18, cu12, cu6), by(cd18, cd12, cd6), by(gcu18, gcu12, gcu6), by(gcd18, gcd12, gcd6)
    HU, HD, GHU, GHD = by(hu18, hu12, hu6), by(hd18, hd12, hd6), by(ghu18, ghu12, ghu6), by(ghd18, ghd12, ghd6)
    SO, SI, RO, RI = by(so18, so12, so6), by(si18, si12, si6), by(ro18, ro12, ro6), by(ri18, ri12, ri6)
    IU, ID = by(iu18, iu12, iu6), by(id18, id12, id6)
    RATE_HBM = {18: w18_hbm, 12: w12_hbm, 6: w6_hbm}

    def start_weights(step):
        for k, tap in enumerate(ORDER[step]):
            src = wp_hbm if tap is None else RATE_HBM[tap[0]].at[tap[1], tap[2]]
            pltpu.make_async_copy(src, w.at[step, k], wsem.at[step]).start()

    start_weights(0)
    xcopies = []
    part = PIX // XPARTS
    for i in range(XPARTS):
        cp = pltpu.make_async_copy(x_hbm.at[pl.ds(part * i, part)], x.at[pl.ds(part * i, part)], xsem.at[i])
        cp.start()
        xcopies.append(cp)
    late = [pltpu.make_async_copy(wpool_hbm, wpool, wpsem.at[0]), pltpu.make_async_copy(wproj_hbm, wproj, wpsem.at[1])]

    barrier = pltpu.get_barrier_semaphore()
    for k in range(1, n_row):
        pl.semaphore_signal(barrier, inc=1, device_id=(lax.rem(r + k, n_row), c), device_id_type=MESH)
    for k in range(1, n_col):
        pl.semaphore_signal(barrier, inc=1, device_id=(r, lax.rem(c + k, n_col)), device_id_type=MESH)

    for there, bufs in ((has_up, (GCD, GHD)), (has_down, (GCU, GHU)), (has_outer, (RO,))):
        @pl.when(jnp.logical_not(there))
        def _(bufs=bufs):
            for buf in bufs:
                for d in RATES:
                    buf[d][...] = jnp.zeros_like(buf[d])

    chans = x.shape[1]
    lanes = chans // BR
    share = chans // n_row

    def remote(src, dst, sems, n, to):
        return pltpu.make_async_remote_copy(
            src_ref=src, dst_ref=dst, send_sem=sems[0].at[n], recv_sem=sems[1].at[n],
            device_id=to, device_id_type=MESH)

    def share_copy(k):
        to = lax.rem(r + k, n_row)
        return remote(shares.at[to], got_shares.at[k], (ps_ss, ps_rs), k, (to, c))

    def sum_copy(k):
        return remote(sums.at[0], sums.at[k], (pc_ss, pc_rs), k, (r, lax.rem(c + k, n_col)))

    def product_copy(k):
        return remote(products.at[0], products.at[k], (pp_ss, pp_rs), k, (lax.rem(r + k, n_row), c))

    def corner_copies(d):
        n = 2 * RATES.index(d)
        return (lambda: remote(CU[d], GCU[d], (row_ss, row_rs), n, (up, c)),
                lambda: remote(CD[d], GCD[d], (row_ss, row_rs), n + 1, (down, c)))

    def own_copies(d):
        n = 2 * RATES.index(d)
        return (lambda: remote(HU[d], GHU[d], (own_ss, own_rs), n, (up, c)),
                lambda: remote(HD[d], GHD[d], (own_ss, own_rs), n + 1, (down, c)))

    def side_copies(d):
        n = 2 * RATES.index(d)
        return (lambda: remote(SO[d], RO[d], (col_ss, col_rs), n, (r, outer)),
                lambda: remote(SI[d], RI[d], (col_ss, col_rs), n + 1, (r, inner)))

    def inner_copies(d):
        n = 2 * RATES.index(d)
        high = up8(d)
        at = (1 - core) * (COLS + d)
        src_u = z.at[pl.ds(BASE[d] + 2 * PLANE[d] + at, d), pl.ds(0, high)]
        src_d = z.at[pl.ds(BASE[d] + at, d), pl.ds(ROWS - high, high)]
        return (lambda: remote(src_u, IU[d], (in_ss, in_rs), n, (r, inner)),
                lambda: remote(src_d, ID[d], (in_ss, in_rs), n + 1, (r, inner)))

    def start_rows(copies):
        @pl.when(has_up)
        def _():
            copies[0]().start()

        @pl.when(has_down)
        def _():
            copies[1]().start()

    def arrive_rows(copies):
        @pl.when(has_down)
        def _():
            copies[0]().wait_recv()

        @pl.when(has_up)
        def _():
            copies[1]().wait_recv()

    def pack(d, at, count, to_up, to_down):
        g = PACK[d]
        for k in range(0, count, g):
            n = min(g, count - k)
            gap = [jnp.zeros((up16(n * d) - n * d, BR), F32)] if n * d % 16 else []
            rows = slice(k * d, k * d + up16(n * d))
            tops = [z[BASE[d] + 2 * PLANE[d] + at + k + j][0:d] for j in range(n)]
            ends = [z[BASE[d] + at + k + j][ROWS - d : ROWS] for j in range(n)]
            to_up[rows] = jnp.concatenate(tops + gap, axis=0).astype(BF)
            to_down[rows] = jnp.concatenate(ends + gap, axis=0).astype(BF)

    def summed(d, at, count, got=None, k=0):
        if got is None:
            got_u = got_d = jnp.zeros((count * d, BR), F32)
        else:
            got_u, got_d = (take(buf[d], k * d, (k + count) * d) for buf in got)
        above, below, same = [], [], []
        for j in range(count):
            z0, z1, z2 = (z[BASE[d] + a * PLANE[d] + at + j] for a in range(3))
            above += [got_d[j * d : (j + 1) * d], z0[0 : ROWS - d]]
            below += [z2[d:ROWS], got_u[j * d : (j + 1) * d]]
            same.append(z1)
        return sum(jnp.concatenate(parts, axis=0) for parts in (same, above, below))

    def corners_out(d):
        pack(d, core * (COLS + d), d, CU[d], CD[d])
        start_rows(corner_copies(d))
        for copy in inner_copies(d):
            copy().start()

    def own_arrive(d):
        for copy in inner_copies(d):
            copy().wait_recv()

    def own_pack(d):
        high = up8(d)
        at = d + (1 - core) * (COLS - d)
        row = lax.broadcasted_iota(jnp.int32, (d, high, BR), 1)
        z[pl.ds(BASE[d] + 2 * PLANE[d] + at, d), 0:high] += jnp.where(row < d, IU[d][...], 0.0)
        z[pl.ds(BASE[d] + at, d), ROWS - high : ROWS] += jnp.where(row >= high - d, ID[d][...], 0.0)
        pack(d, d, COLS, HU[d], HD[d])

    def inner_side(d):
        at = (1 - core) * (COLS + d)
        for k in range(0, d, 6):
            SI[d][ROWS * k : ROWS * (k + 6)] = summed(d, at + k, 6).astype(BF)
        side_copies(d)[1]().start()

    def outer_side(d):
        at = core * (COLS + d)
        for k in range(0, d, 6):
            SO[d][ROWS * k : ROWS * (k + 6)] = summed(d, at + k, 6, (GCU, GCD), k).astype(BF)

        @pl.when(has_outer)
        def _():
            side_copies(d)[0]().start()

    def own_in(d):
        for k in range(0, COLS, 4):
            at = BASE[d] + PLANE[d] + d + k
            z[at : at + 4] = summed(d, d + k, 4, (GHU, GHD), k).reshape(4, ROWS, BR)

    def pixel_sum():
        for k in range(lanes):
            acc = jnp.zeros((8, BR), F32)
            for at in range(0, PIX, 16):
                rows = x[at : at + 16, BR * k : BR * k + BR].astype(F32)
                acc = acc + (rows[0:8] + rows[8:16])
            n, at = divmod(BR * k, share)
            shares[n, :, at : at + BR] = jnp.sum(acc, axis=0, keepdims=True)

    def pool_first():
        for k in range(1, n_row):
            share_copy(k).start()

    def pool_second():
        for k in range(1, n_row):
            share_copy(k).wait_recv()
        acc = shares[r]
        for k in range(1, n_row):
            acc = acc + got_shares[k]
        sums[0] = acc
        for k in range(1, n_col):
            sum_copy(k).start()

    def pool_third():
        for k in range(1, n_col):
            sum_copy(k).wait_recv()
        acc = sums[0]
        for k in range(1, n_col):
            acc = acc + sums[k]
        pooled = (acc / (PIX * n_row * n_col)).astype(BF).astype(F32)
        parts = jnp.zeros((8, BR), F32)
        for k in range(share // BR):
            side = jnp.transpose(jnp.broadcast_to(pooled[:, BR * k : BR * k + BR], (8, BR)), (1, 0))[:, 0:1]
            rows = wpool[pl.ds(pl.multiple_of(r * share + BR * k, BR), BR)]
            parts = parts + jnp.sum((side * rows.astype(F32)).reshape(BR // 8, 8, BR), axis=0)
        products[0] = jnp.sum(parts, axis=0, keepdims=True)
        for k in range(1, n_row):
            product_copy(k).start()

    def pool_fourth():
        for k in range(1, n_row):
            product_copy(k).wait_recv()
        acc = products[0]
        for k in range(1, n_row):
            acc = acc + products[k]
        branch = jnp.broadcast_to(jnp.maximum(acc, 0.0), (16, BR)).astype(BF)
        return jnp.dot(branch, wproj[4 * BR : 5 * BR], preferred_element_type=F32)[0:1]

    filled = set()

    def put(at, y):
        cols = y.shape[0] // ROWS
        y = y.reshape(cols, ROWS, BR)
        k = 0
        while k < cols:
            old = at + k in filled
            n = 1
            while k + n < cols and (at + k + n in filled) == old:
                n += 1
            if old:
                z[at + k : at + k + n] += y[k : k + n]
            else:
                z[at + k : at + k + n] = y[k : k + n]
            k += n
        filled.update(range(at, at + cols))

    def weights_in(step):
        pltpu.make_async_copy(w.at[step], w.at[step], wsem.at[step]).wait()
        if 0 < step < STEPS - 2:
            start_weights(step + 2)
        if step == 2:
            for copy in late:
                copy.start()

    def multiply(step, first=None):
        taps = jnp.concatenate([w[step, k] for k in range(TAPS)], axis=1)
        half = PIX // 2
        if first is None:
            y = jnp.concatenate(
                [jnp.dot(x[at : at + half], taps, preferred_element_type=F32) for at in (0, half)], axis=0)
        else:
            y = jnp.dot(x[first : first + half], taps, preferred_element_type=F32)
        for k, tap in enumerate(ORDER[step]):
            at = POINT
            if tap is not None:
                d, a, b = tap
                at = BASE[d] + a * PLANE[d] + (2 - b) * d
            put(at + (first or 0) // ROWS, y[:, BR * k : BR * k + BR])

    hole = BASE[18] + PLANE[18] + COLS
    z[hole : hole + 36 - COLS] = jnp.zeros((36 - COLS, ROWS, BR), F32)
    filled.update(range(hole, hole + 36 - COLS))

    xcopies[0].wait()
    weights_in(0)
    start_weights(1)
    multiply(0, 0)
    xcopies[1].wait()
    start_weights(2)
    pixel_sum()
    multiply(0, PIX // 2)
    pl.semaphore_wait(barrier, n_row + n_col - 2)
    weights_in(1)
    pool_first()
    corners_out(18)
    multiply(1)
    own_arrive(18)
    weights_in(2)
    own_pack(18)
    start_rows(own_copies(18))
    multiply(2)
    corners_out(12)
    pool_second()
    arrive_rows(corner_copies(18))
    weights_in(3)
    weights_in(4)
    outer_side(18)
    inner_side(18)
    multiply(3)
    corners_out(6)
    multiply(4)
    own_arrive(12)
    arrive_rows(corner_copies(12))
    weights_in(5)
    outer_side(12)
    own_pack(12)
    start_rows(own_copies(12))
    inner_side(12)
    arrive_rows(own_copies(18))
    own_in(18)
    multiply(5)
    for copy in late:
        copy.wait()
    pool_third()
    own_arrive(6)
    arrive_rows(corner_copies(6))
    weights_in(6)
    own_pack(6)
    start_rows(own_copies(6))
    outer_side(6)
    inner_side(6)
    multiply(6)
    arrive_rows(own_copies(12))
    own_in(12)
    arrive_rows(own_copies(6))
    own_in(6)
    pool_part = pool_fourth()
    joined[:, 0:BR] = jnp.maximum(z[POINT : POINT + COLS], 0.0).reshape(PIX, BR).astype(BF)

    for n, d in ((3, 18), (2, 12), (1, 6)):
        side_copies(d)[1]().wait_recv()

        @pl.when(has_outer)
        def _(d=d):
            side_copies(d)[0]().wait_recv()

        at = BASE[d] + PLANE[d] + d
        for buf, side in ((RO[d], core), (RI[d], 1 - core)):
            z[pl.ds(at + side * (COLS - d), d)] += buf[...].astype(F32).reshape(d, ROWS, BR)
        joined[:, BR * n : BR * (n + 1)] = jnp.maximum(z[at : at + COLS], 0.0).reshape(PIX, BR).astype(BF)

    for at in (0, PIX // 2):
        rows = slice(at, at + PIX // 2)
        mixed = jnp.dot(joined[rows], wproj[0 : 4 * BR], preferred_element_type=F32)
        out_ref[rows] = jnp.maximum(mixed + pool_part, 0.0).astype(BF)

    for k in range(1, n_row):
        share_copy(k).wait_send()
        product_copy(k).wait_send()
    for k in range(1, n_col):
        sum_copy(k).wait_send()
    for d in RATES:
        inner_copies(d)[0]().wait_send()
        inner_copies(d)[1]().wait_send()
        side_copies(d)[1]().wait_send()
        for there, copy in (
            (has_up, corner_copies(d)[0]), (has_down, corner_copies(d)[1]),
            (has_up, own_copies(d)[0]), (has_down, own_copies(d)[1]), (has_outer, side_copies(d)[0]),
        ):
            @pl.when(there)
            def _(copy=copy):
                copy().wait_send()


def per_device(n_row, n_col, features, w_point, w_rate_six, w_rate_twelve, w_rate_eighteen, w_pool, w_proj):
    chans = features.shape[2]
    vm = pltpu.VMEM
    dma = pltpu.SemaphoreType.DMA
    scratch = [vm((PIX, chans), BF), vm((STEPS, TAPS, chans, BR), BF), vm((chans, BR), BF), vm((5 * BR, OUT), BF)]
    scratch += [vm((POINT + COLS, ROWS, BR), F32), vm((PIX, 4 * BR), BF)]
    for size in (lambda d: up16(d * d), lambda d: up16(COLS * d), lambda d: ROWS * d):
        for _ in range(4):
            scratch += [vm((size(d), BR), BF) for d in RATES]
    for _ in range(2):
        scratch += [vm((d, up8(d), BR), F32) for d in RATES]
    share = chans // n_row
    scratch += [vm((n_row, 1, share), F32), vm((n_row, 1, share), F32), vm((n_col, 1, share), F32), vm((n_row, 1, BR), F32)]
    scratch += [dma((XPARTS,)), dma((STEPS,)), dma((2,))] + [dma((6,))] * 8
    scratch += [dma((n_row,)), dma((n_row,)), dma((n_col,)), dma((n_col,)), dma((n_row,)), dma((n_row,))]
    pixels = jnp.transpose(features, (1, 0, 2)).reshape(PIX, chans)
    out = pl.pallas_call(
        functools.partial(body, n_row, n_col),
        name="aspp_branches",
        out_shape=jax.ShapeDtypeStruct((PIX, OUT), BF),
        in_specs=[pl.BlockSpec(memory_space=pltpu.HBM)] * 7,
        out_specs=pl.BlockSpec(memory_space=pltpu.VMEM),
        scratch_shapes=scratch,
        compiler_params=pltpu.CompilerParams(
            collective_id=0, has_side_effects=True, vmem_limit_bytes=48 << 20),
        cost_estimate=pl.CostEstimate(
            flops=2 * PIX * chans * BR * 28, bytes_accessed=20 << 20, transcendentals=0),
    )(*[pltpu.with_memory_space_constraint(a, pltpu.HBM) for a in (
        pixels, w_point, w_rate_six, w_rate_twelve, w_rate_eighteen, w_pool, w_proj)])
    return jnp.transpose(out.reshape(COLS, ROWS, OUT), (1, 0, 2))


def solution(mesh):
    placed = (P("row", "col", None), P(), P(), P(), P(), P(), P())
    return jax.shard_map(
        functools.partial(per_device, mesh.shape["row"], mesh.shape["col"]),
        mesh=mesh, in_specs=placed, out_specs=P("row", "col", None), check_vma=False)
```
